32 devices in a mesh: dom: 8 (over z, y), scen: 4 (over x, core).
Axes of the slice: x: 2, y: 2, z: 4, core: 2. Of those that a mesh axis runs over, the one named last changes fastest.
Arguments:
- embedding: bfloat16 [81920, 256], P(('dom', 'scen')), may hold values from -6 to 6
- scenario_feats: bfloat16 [16, 81920], P(None, ('dom', 'scen')), may hold values from -6 to 6
- adjacency: bfloat16 [640, 2, 128, 128], P(('dom', 'scen')), may hold values from -0.3125 to 0.3125
- driver_weight: bfloat16 [81920, 128], P(('dom', 'scen')), may hold values from -0.3125 to 0.3125
- local_slot: int32 [640], P(('dom', 'scen')), may hold values from 0 to 79, as said below
- halo_slot: int32 [640], P(('dom', 'scen')), may hold values from 0 to 15, as said below
- send_rows: int32 [256, 256], P(('dom', 'scen')), may hold values from 0 to 2559
- send_count: int32 [256], P(('dom', 'scen')), may hold values from 1 to 256, as said below
- hot_ids: int32 [128], replicated, may hold values from 0 to 81919, as said below
- first_weight: bfloat16 [512, 256], P('scen'), may hold values from -0.25 to 0.25
- feature_weight: bfloat16 [16, 256], replicated, may hold values from -1.5 to 1.5
- first_bias: float32 [256], replicated, may hold values from -3 to 3
- second_weight: bfloat16 [256, 256], P('scen'), may hold values from -0.375 to 0.375
- second_bias: float32 [256], replicated, may hold values from -3 to 3
Outputs:
- updated: bfloat16 [81920, 256], P(('dom', 'scen'))
The draws below stay inside these ranges and needn't reach their ends.
Inputs may be any that keep to these rules, and one draw needn't show every extreme that they name: `local_slot`: the 20 entries of one device are distinct and name exactly 5 tiles of each device of its partition; values s * 20 to s * 20 + 19 are tiles of scen index s. `halo_slot`: the entries of one device name every halo tile at least once. `send_count`: every device has a partition to which it sends 256 pins. `hot_ids`: no device holds more than 4 of them, and some device holds exactly that many.
All inputs are finite; a program needn't handle non-finite values.
Results may differ from the reference program's by a relative error of at most 0.0038.
Values may be sent and summed in bfloat16 or wider, within the bound.
A program may use at most 64 MiB of HBM per device.

```python
import jax
import jax.numpy as jnp
from jax import lax

WIDTH = 256
FEAT = 16
TILE = 128
HOT = 128
HALO_TILES = 16
TILES = 20
ROWS = 2560
PINS = 81920
CAP = 256
LOCAL_CAP = 5
N_DOM = 8
N_SCEN = 4
DEVICES = 32


def draw_local_slot(key, part):
    keys = jax.random.split(jax.random.fold_in(key, 11), DEVICES * N_SCEN)
    picks = jax.vmap(lambda k: jax.random.permutation(k, TILES)[:LOCAL_CAP])(keys)
    picks = picks.reshape(DEVICES, N_SCEN, LOCAL_CAP) + (jnp.arange(N_SCEN, dtype=jnp.int32) * TILES)[None, :, None]
    picks = picks.reshape(DEVICES, TILES)
    orders = jax.random.split(jax.random.fold_in(key, 12), DEVICES)
    mixed = jax.vmap(lambda k, r: jax.random.permutation(k, r))(orders, picks)
    return mixed.reshape(-1).astype(jnp.int32)


def draw_halo_slot(key, part):
    keys = jax.random.split(jax.random.fold_in(key, 21), DEVICES)

    def single(k):
        first, second, third = jax.random.split(k, 3)
        base = jax.random.permutation(first, HALO_TILES)
        extra = jax.random.randint(second, (TILES - HALO_TILES,), 0, HALO_TILES)
        return jax.random.permutation(third, jnp.concatenate([base, extra]))
    return jax.vmap(single)(keys).reshape(-1).astype(jnp.int32)


def draw_send_count(key, part):
    first, second = jax.random.split(jax.random.fold_in(key, 31))
    counts = jax.random.randint(first, (DEVICES, N_DOM), 1, CAP + 1)
    fullest = jax.random.randint(second, (DEVICES,), 0, N_DOM)
    counts = jnp.where(jnp.arange(N_DOM)[None, :] == fullest[:, None], CAP, counts)
    return counts.reshape(-1).astype(jnp.int32)


def draw_hot_ids(key, part):
    first, second = jax.random.split(jax.random.fold_in(key, 41))
    owners = jax.random.permutation(first, DEVICES)[jnp.arange(HOT) % DEVICES]
    within = jax.random.randint(second, (HOT,), 0, ROWS)
    return (owners * ROWS + within).astype(jnp.int32)


def place_ends(entries, own_key, low, top_value):
    dims = entries.shape
    place = [jax.random.randint(jax.random.fold_in(own_key, axis), (), 0, dims[axis]) for axis in range(len(dims))]
    entries = entries.at[tuple(place)].set(low)
    longest = dims.index(max(dims))
    place[longest] = (place[longest] + 1) % dims[longest]
    return entries.at[tuple(place)].set(top_value)


def steps_of(stream_key, extent, cuts, low, largest):
    level, own = 1.0, jax.random.fold_in(stream_key, 6)
    for axis_at, blocks in cuts:
        draws = jnp.exp(jax.random.uniform(jax.random.fold_in(own, axis_at), (blocks,), jnp.float32, low / len(cuts), largest / len(cuts)))
        level = level * jnp.repeat(draws, extent[axis_at] // blocks).reshape([-1 if axis == axis_at else 1 for axis in range(len(extent))])
    return level


def centred(stream_key, extent, width, most, cuts=(), kind=jnp.bfloat16):
    values = width * jax.random.normal(stream_key, extent, jnp.float32)
    if cuts:
        values = values * steps_of(stream_key, extent, cuts, -0.22, 0.18)
    return jnp.clip(values, -most, most).astype(kind)


def setup_inputs(seed: int = 0) -> dict:
    key_list = jax.random.split(jax.random.key(seed), 15)
    embedding = centred(key_list[0], (PINS, WIDTH), 1.0, 6.0, ((0, 32),))
    scenario_feats = centred(key_list[1], (FEAT, PINS), 1.0, 6.0, ((1, 32),))
    adjacency = centred(key_list[2], (PINS // TILE, 2, TILE, TILE), (3 * TILE) ** -0.5, 0.3125, ((0, 32),))
    driver_weight = centred(key_list[3], (PINS, HOT), (3 * TILE) ** -0.5, 0.3125, ((0, 32),))
    local_slot = draw_local_slot(jax.random.fold_in(key_list[14], 71), 0)
    halo_slot = draw_halo_slot(jax.random.fold_in(key_list[14], 71), 0)
    send_rows = place_ends(jax.random.randint(key_list[6], (DEVICES * N_DOM, CAP), 0, ROWS), jax.random.fold_in(key_list[6], 1), 0, ROWS - 1).astype(jnp.int32)
    send_count = draw_send_count(jax.random.fold_in(key_list[14], 71), 0)
    hot_ids = draw_hot_ids(jax.random.fold_in(key_list[14], 71), 0)
    first_weight = centred(key_list[9], (2 * WIDTH, WIDTH), (2 * WIDTH) ** -0.5, 0.25, ((0, 4),))
    feature_weight = centred(key_list[10], (FEAT, WIDTH), FEAT ** -0.5, 1.5)
    first_bias = centred(key_list[11], (WIDTH,), 0.5, 3.0, (), jnp.float32)
    second_weight = centred(key_list[12], (WIDTH, WIDTH), WIDTH ** -0.5, 0.375, ((0, 4),))
    second_bias = centred(key_list[13], (WIDTH,), 0.5, 3.0, (), jnp.float32)
    return dict(embedding=embedding, scenario_feats=scenario_feats, adjacency=adjacency, driver_weight=driver_weight, local_slot=local_slot, halo_slot=halo_slot, send_rows=send_rows, send_count=send_count, hot_ids=hot_ids, first_weight=first_weight, feature_weight=feature_weight, first_bias=first_bias, second_weight=second_weight, second_bias=second_bias)


def reference(embedding, scenario_feats, adjacency, driver_weight, local_slot, halo_slot, send_rows, send_count, hot_ids, first_weight, feature_weight, first_bias, second_weight, second_bias):
    rows = TILES * TILE
    drivers = embedding[hot_ids]
    send_view = send_rows.reshape(DEVICES, N_DOM, CAP)
    count_view = send_count.reshape(DEVICES, N_DOM)

    def device(index):
        domain = index // N_SCEN
        group = index - domain * N_SCEN
        own = lax.dynamic_slice_in_dim(embedding, index * rows, rows, 0)
        partition = lax.dynamic_slice_in_dim(embedding, domain * N_SCEN * rows, N_SCEN * rows, 0).reshape(N_SCEN * TILES, TILE, WIDTH)
        slots = lax.dynamic_slice_in_dim(local_slot, index * TILES, TILES, 0)
        local_tiles = partition[slots].astype(jnp.float32)
        peers = jnp.arange(N_DOM, dtype=jnp.int32) * N_SCEN + group
        chosen = send_view[peers, domain]
        counts = count_view[peers, domain]
        live = jnp.arange(CAP, dtype=jnp.int32)[None, :] < counts[:, None]
        flat = (peers[:, None] * rows + chosen).astype(jnp.int32)
        halo = jnp.where(live[:, :, None], embedding[flat].astype(jnp.float32), jnp.float32(0.0))
        halo = halo.reshape(HALO_TILES, TILE, WIDTH)
        halo_tiles = halo[lax.dynamic_slice_in_dim(halo_slot, index * TILES, TILES, 0)]
        blocks = lax.dynamic_slice_in_dim(adjacency, index * TILES, TILES, 0).astype(jnp.float32)
        summed = jnp.einsum("tij,tjc->tic", blocks[:, 0], local_tiles)
        summed = summed + jnp.einsum("tij,tjc->tic", blocks[:, 1], halo_tiles)
        weights_hot = lax.dynamic_slice_in_dim(driver_weight, index * rows, rows, 0)
        summed = summed.reshape(rows, WIDTH) + jnp.dot(weights_hot, drivers, preferred_element_type=jnp.float32)
        aggregate = summed.astype(jnp.bfloat16)
        joined = jnp.concatenate([own, aggregate], axis=1)
        feats = lax.dynamic_slice_in_dim(scenario_feats, index * rows, rows, 1)
        inner = jnp.dot(joined, first_weight, preferred_element_type=jnp.float32)
        inner = inner + jnp.dot(feats.T, feature_weight, preferred_element_type=jnp.float32) + first_bias
        activated = jax.nn.gelu(inner, approximate=False).astype(jnp.bfloat16)
        result = own.astype(jnp.float32) + jnp.dot(activated, second_weight, preferred_element_type=jnp.float32) + second_bias
        return result.astype(jnp.bfloat16)

    outputs = lax.map(device, jnp.arange(DEVICES, dtype=jnp.int32))
    return outputs.reshape(DEVICES * rows, WIDTH)
```

```python
import functools

import jax
import jax.numpy as jnp
from jax import lax
from jax.experimental import pallas as pl
from jax.experimental.pallas import tpu as pltpu
from jax.sharding import PartitionSpec as P

MESH = pl.DeviceIdType.MESH
LANES = 128
GROUP = 256
PAD = 16


def flipped(index, mask):
    bit = 1
    while bit <= mask:
        if mask & bit:
            index = index + bit * (1 - 2 * ((index // bit) % 2))
        bit *= 2
    return index


def spread(row):
    across = jnp.broadcast_to(row.astype(jnp.float32), (LANES, LANES))
    return across, across.T


def whole_part(values, size):
    return jnp.floor((values + 0.5) * (1.0 / size))


def iota_f32(shape, dim):
    return lax.broadcasted_iota(jnp.int32, shape, dim).astype(jnp.float32)


def picked_rows(column, emb_ref):
    tiles, tile, width = emb_ref.shape
    rows = tiles * tile
    lane = iota_f32(column.shape, 1)
    blocks = [
        jnp.where(column == lane + float(at), 1.0, 0.0).astype(jnp.bfloat16)
        for at in range(0, rows, LANES)
    ]
    return jnp.dot(
        jnp.concatenate(blocks, axis=1),
        emb_ref[...].reshape(rows, width),
        preferred_element_type=jnp.float32,
    ).astype(jnp.bfloat16)


def exchange_kernel(
    n_dom,
    n_scen,
    hot_ref,
    slot_ref,
    rows_ref,
    count_ref,
    emb_ref,
    w1_ref,
    w2_ref,
    halo_ref,
    local_ref,
    drv_ref,
    w1f_ref,
    w2f_ref,
    keys_ref,
    out_buf,
    stage,
    myreq,
    reqs,
    reqs_smem,
    mine,
    gat1,
    gat2,
    padrow,
    halo_send,
    halo_recv,
    req_send,
    req_recv,
    loc_send,
    loc_recv,
    d1_send,
    d1_recv,
    d2_send,
    d2_recv,
    w1_send,
    w1_recv,
    w2_send,
    w2_recv,
    own_sem,
):
    d = lax.axis_index("dom")
    s = lax.axis_index("scen")
    tiles, tile, _ = emb_ref.shape
    rows = tiles * tile
    per = tiles // n_scen
    cap = halo_ref.shape[0] // n_dom
    per_group = max(1, GROUP // cap)
    n_groups = n_dom // per_group
    drv_rows = n_dom * PAD

    def dom_peers(body):
        def step(k, carry):
            body(lax.rem(d + k, n_dom))
            return carry

        lax.fori_loop(1, n_dom, step, 0)

    def scen_peers(body):
        for k in range(n_scen - 1, 0, -1):
            body(flipped(s, k))

    def remote(src, dst, send, recv, where):
        return pltpu.make_async_remote_copy(
            src_ref=src,
            dst_ref=dst,
            send_sem=send,
            recv_sem=recv,
            device_id=where,
            device_id_type=MESH,
        )

    def block(ref, index, size):
        return ref.at[pl.ds(pl.multiple_of(index * size, size), size)]

    def halo_copy(peer, mark):
        return remote(
            block(out_buf, peer, cap),
            block(halo_ref, mark, cap),
            halo_send.at[peer],
            halo_recv.at[mark],
            {"dom": peer},
        )

    def req_copy(peer, mark):
        return remote(myreq, reqs.at[mark], req_send.at[peer], req_recv.at[mark], {"scen": peer})

    def loc_copy(peer, mark):
        return remote(
            block(stage, peer, per * tile),
            block(local_ref, mark, per * tile),
            loc_send.at[peer],
            loc_recv.at[mark],
            {"scen": peer},
        )

    def d1_copy(peer, mark):
        return remote(
            mine, block(gat1, mark, PAD), d1_send.at[peer], d1_recv.at[mark], {"dom": peer}
        )

    def d2_copy(peer, mark):
        return remote(
            gat1, block(gat2, mark, drv_rows), d2_send.at[peer], d2_recv.at[mark], {"scen": peer}
        )

    def w1_copy(peer, mark):
        return remote(
            w1_ref,
            block(w1f_ref, mark, w1_ref.shape[0]),
            w1_send.at[peer],
            w1_recv.at[mark],
            {"scen": peer},
        )

    def w2_copy(peer, mark):
        return remote(
            w2_ref,
            block(w2f_ref, mark, w2_ref.shape[0]),
            w2_send.at[peer],
            w2_recv.at[mark],
            {"scen": peer},
        )

    barrier = pltpu.get_barrier_semaphore()
    dom_peers(
        lambda p: pl.semaphore_signal(
            barrier, inc=1, device_id={"dom": p}, device_id_type=MESH
        )
    )
    scen_peers(
        lambda u: pl.semaphore_signal(
            barrier, inc=1, device_id={"scen": u}, device_id_type=MESH
        )
    )

    square = (LANES, LANES)
    lane = iota_f32(square, 1)
    sub = iota_f32(square, 0)

    padrow[...] = jnp.full(padrow.shape, -1, jnp.int32)
    padrow[0:1, 0:tiles] = slot_ref[...]
    across = jnp.broadcast_to(padrow[0:1, :], square)
    down = across.T
    ilane = lax.broadcasted_iota(jnp.int32, square, 1)
    isub = lax.broadcasted_iota(jnp.int32, square, 0)

    def holder(slots):
        found = jnp.where(slots >= 0, 0, -1)
        for u in range(1, n_scen):
            found = found + jnp.where(slots >= u * tiles, 1, 0)
        return found

    own_a, own_d = holder(across), holder(down)
    same = own_a == own_d
    rank_col = jnp.sum(jnp.where(same & (ilane < isub), 1, 0), axis=1, keepdims=True)
    rank_row = jnp.sum(jnp.where(same & (isub < ilane), 1, 0), axis=0, keepdims=True)
    key_col = jnp.where(isub < tiles, own_d * per + rank_col, -1)
    wanted = jnp.sum(
        jnp.where(key_col == ilane, down - own_d * tiles, 0), axis=0, keepdims=True
    )
    myreq[...] = jnp.broadcast_to(wanted, myreq.shape)
    keys_ref[...] = jnp.broadcast_to(own_a[0:1, :] * per + rank_row, keys_ref.shape)

    pl.semaphore_wait(barrier, n_dom - 1 + n_scen - 1)
    scen_peers(lambda u: req_copy(u, s).start())

    def row_of(index, columns):
        block_of = rows_ref[:, columns]
        at = lax.broadcasted_iota(jnp.int32, block_of.shape, 0)
        return jnp.sum(jnp.where(at == index, block_of, 0), axis=0, keepdims=True)

    def halo_group(group):
        first = group * per_group
        columns = []
        for half in range(GROUP // LANES):
            if cap >= LANES:
                parts = cap // LANES
                assert per_group == 1 and parts == GROUP // LANES
                row = row_of(first, slice(half * LANES, (half + 1) * LANES))
                limit = count_ref[first]
                place = lax.broadcasted_iota(jnp.int32, (1, LANES), 1) + half * LANES
                row = jnp.where(place < limit, row, -1)
            else:
                parts = LANES // cap
                row = row_of(group * (GROUP // LANES) + half, slice(0, LANES))
                place = lax.broadcasted_iota(jnp.int32, (1, LANES), 1)
                live = place < 0
                for i in range(parts):
                    limit = count_ref[first + half * parts + i]
                    live = live | ((place >= i * cap) & (place < i * cap + limit) & (place < (i + 1) * cap))
                row = jnp.where(live, row, -1)
            columns.append(spread(row)[1])
        block(out_buf, group, GROUP)[...] = picked_rows(
            jnp.concatenate(columns, axis=0), emb_ref
        )

    def halo_start(group):
        halo_group(group)
        if per_group == 1:
            halo_copy(group, d).start()
            return

        def step(i, carry):
            p = group * per_group + i

            @pl.when(p != d)
            def _():
                halo_copy(p, d).start()

            return carry

        lax.fori_loop(0, per_group, step, 0)

    my_group = d // per_group
    order = list(range(n_groups - 1, 0, -1))
    halo_start(flipped(my_group, order[0]))

    r_ids, c_ids = spread(hot_ref[...])
    r_own, c_own = whole_part(r_ids, rows), whole_part(c_ids, rows)
    equal = r_ids == c_ids
    new_col = 1.0 - jnp.max(jnp.where(equal & (lane < sub), 1.0, 0.0), axis=1, keepdims=True)
    new_row = 1.0 - jnp.max(jnp.where(equal & (sub < lane), 1.0, 0.0), axis=0, keepdims=True)
    alike = r_own == c_own
    hot_rank_row = jnp.sum(
        jnp.where(alike & (c_ids < r_ids), new_col, 0.0), axis=0, keepdims=True
    )
    hot_rank_col = jnp.sum(
        jnp.where(alike & (r_ids < c_ids), new_row, 0.0), axis=1, keepdims=True
    )
    me = (d * n_scen + s).astype(jnp.float32)
    own_rows = picked_rows(c_ids - me * float(rows), emb_ref)
    chosen = jnp.where(
        (iota_f32((PAD, LANES), 0) == hot_rank_row) & (r_own[0:1, :] == me), new_row, 0.0
    ).astype(jnp.bfloat16)
    mine[...] = jnp.dot(chosen, own_rows, preferred_element_type=jnp.float32).astype(jnp.bfloat16)
    block(gat1, d, PAD)[...] = mine[...]
    dom_peers(lambda p: d1_copy(p, d).start())

    halo_start(flipped(my_group, order[1]))

    scen_peers(lambda u: req_copy(u, u).wait_recv())
    reqs[pl.ds(s, 1)] = myreq[...][None]
    fetch = pltpu.make_async_copy(reqs, reqs_smem, own_sem.at[0])
    fetch.start()
    fetch.wait()

    def stage_for(u):
        for r in range(per):
            slot = reqs_smem[u, 0, s * per + r]
            block(stage, u * per + r, tile)[...] = emb_ref[slot]

    def serve(u):
        stage_for(u)
        loc_copy(u, s).start()

    scen_peers(serve)
    scen_peers(lambda u: w1_copy(u, s).start())
    scen_peers(lambda u: w2_copy(u, s).start())
    stage_for(s)
    own_copies = [
        pltpu.make_async_copy(
            block(stage, s, per * tile), block(local_ref, s, per * tile), own_sem.at[0]
        ),
        pltpu.make_async_copy(w1_ref, block(w1f_ref, s, w1_ref.shape[0]), own_sem.at[1]),
        pltpu.make_async_copy(w2_ref, block(w2f_ref, s, w2_ref.shape[0]), own_sem.at[2]),
    ]
    for copy in own_copies:
        copy.start()

    for mask in order[2:]:
        halo_start(flipped(my_group, mask))
    if per_group == 1:
        halo_group(my_group)
    else:
        halo_start(my_group)
    own_halo = pltpu.make_async_copy(
        block(out_buf, d, cap), block(halo_ref, d, cap), own_sem.at[3]
    )
    own_halo.start()

    dom_peers(lambda p: d1_copy(p, p).wait_recv())
    scen_peers(lambda u: d2_copy(u, s).start())
    block(gat2, s, drv_rows)[...] = gat1[...]
    scen_peers(lambda u: d2_copy(u, u).wait_recv())
    c_dom = whole_part(c_own, n_scen)
    place = (c_own - c_dom * float(n_scen)) * float(drv_rows) + c_dom * float(PAD) + hot_rank_col
    total = jnp.zeros(drv_ref.shape, jnp.float32)
    for at in range(0, n_scen * drv_rows, LANES):
        pick = jnp.where(place == lane + float(at), 1.0, 0.0).astype(jnp.bfloat16)
        total += jnp.dot(pick, gat2[at : at + LANES, :], preferred_element_type=jnp.float32)
    drv_ref[...] = total.astype(jnp.bfloat16)

    for copy in own_copies:
        copy.wait()
    own_halo.wait()
    dom_peers(lambda p: d1_copy(p, p).wait_send())
    for make in (req_copy, d2_copy):
        scen_peers(lambda u: make(u, u).wait_send())
    for make in (w1_copy, w2_copy, loc_copy):
        scen_peers(lambda u: make(u, u).wait())
    dom_peers(lambda p: halo_copy(p, p).wait())


def exchange(hot_ids, local_slot, send_rows, send_count, embedding, w1, w2, n_dom, n_scen, tile):
    rows, width = embedding.shape
    slots = send_rows.size
    cap = send_rows.shape[1]
    hot = hot_ids.shape[0]
    assert -(-hot // (n_dom * n_scen)) <= PAD
    if cap < LANES:
        send_rows = send_rows.reshape(-1, LANES)
    vmem = pl.BlockSpec(memory_space=pltpu.VMEM)
    smem = pl.BlockSpec(memory_space=pltpu.SMEM)
    anywhere = pl.BlockSpec(memory_space=pl.ANY)
    bf16 = jnp.bfloat16
    dma = pltpu.SemaphoreType.DMA
    return pl.pallas_call(
        functools.partial(exchange_kernel, n_dom, n_scen),
        out_shape=(
            jax.ShapeDtypeStruct((slots, width), bf16),
            jax.ShapeDtypeStruct((rows, width), bf16),
            jax.ShapeDtypeStruct((hot, width), bf16),
            jax.ShapeDtypeStruct((n_scen * w1.shape[0], width), bf16),
            jax.ShapeDtypeStruct((n_scen * w2.shape[0], width), bf16),
            jax.ShapeDtypeStruct((8, LANES), jnp.int32),
        ),
        in_specs=[vmem, vmem, vmem, smem, vmem, anywhere, anywhere],
        out_specs=(anywhere, anywhere, vmem, anywhere, anywhere, vmem),
        scratch_shapes=[
            pltpu.VMEM((slots, width), bf16),
            pltpu.VMEM((rows, width), bf16),
            pltpu.VMEM((8, LANES), jnp.int32),
            pltpu.VMEM((n_scen, 8, LANES), jnp.int32),
            pltpu.SMEM((n_scen, 8, LANES), jnp.int32),
            pltpu.VMEM((PAD, width), bf16),
            pltpu.VMEM((n_dom * PAD, width), bf16),
            pltpu.VMEM((n_scen * n_dom * PAD, width), bf16),
            pltpu.VMEM((8, LANES), jnp.int32),
            dma((n_dom,)),
            dma((n_dom,)),
            dma((n_scen,)),
            dma((n_scen,)),
            dma((n_scen,)),
            dma((n_scen,)),
            dma((n_dom,)),
            dma((n_dom,)),
            dma((n_scen,)),
            dma((n_scen,)),
            dma((n_scen,)),
            dma((n_scen,)),
            dma((n_scen,)),
            dma((n_scen,)),
            dma((4,)),
        ],
        compiler_params=pltpu.CompilerParams(
            collective_id=0, has_side_effects=True, vmem_limit_bytes=40 * 1024 * 1024
        ),
        name="exchange",
    )(
        hot_ids.reshape(1, -1),
        local_slot.reshape(1, -1),
        send_rows,
        send_count,
        embedding.reshape(-1, tile, width),
        w1,
        w2,
    )


def update_kernel(
    count,
    keys_ref,
    halo_slot_ref,
    emb_ref,
    feats_ref,
    adj_ref,
    dw_ref,
    halo_ref,
    local_ref,
    drv_ref,
    w1_ref,
    fw_ref,
    b1_ref,
    w2_ref,
    b2_ref,
    out_ref,
    agg_ref,
):
    step = pl.program_id(0)
    tile = adj_ref.shape[-1]
    width = emb_ref.shape[1]
    for i in range(count):
        key = keys_ref[0, step * count + i]
        slot = halo_slot_ref[step * count + i]
        local = local_ref[pl.ds(pl.multiple_of(key * tile, tile), tile), :]
        halo = halo_ref[pl.ds(pl.multiple_of(slot * tile, tile), tile), :]
        here = slice(i * tile, (i + 1) * tile)
        total = jnp.dot(adj_ref[i, 0], local, preferred_element_type=jnp.float32)
        total += jnp.dot(adj_ref[i, 1], halo, preferred_element_type=jnp.float32)
        total += jnp.dot(dw_ref[here, :], drv_ref[...], preferred_element_type=jnp.float32)
        agg_ref[here, :] = total.astype(jnp.bfloat16)
    emb = emb_ref[...]
    inner = jnp.dot(emb, w1_ref[:width, :], preferred_element_type=jnp.float32)
    inner += jnp.dot(agg_ref[...], w1_ref[width:, :], preferred_element_type=jnp.float32)
    inner += lax.dot_general(
        feats_ref[...],
        fw_ref[...],
        (((0,), (0,)), ((), ())),
        preferred_element_type=jnp.float32,
    )
    inner += b1_ref[...]
    activated = (0.5 * inner * (1.0 + lax.erf(inner * (0.5**0.5)))).astype(jnp.bfloat16)
    result = jnp.dot(activated, w2_ref[...], preferred_element_type=jnp.float32)
    out_ref[...] = (result + (emb.astype(jnp.float32) + b2_ref[...])).astype(jnp.bfloat16)


def update(keys, halo_slot, embedding, feats, adjacency, dw, halo, local, drv, w1, fw, b1, w2, b2):
    rows, width = embedding.shape
    tiles, _, tile, _ = adjacency.shape
    count = 4 if tiles % 4 == 0 else 1
    part = count * tile

    def all_of(array):
        return pl.BlockSpec(array.shape, lambda i, *_: (0,) * array.ndim)

    b1, b2 = b1.reshape(1, -1), b2.reshape(1, -1)
    grid_spec = pltpu.PrefetchScalarGridSpec(
        num_scalar_prefetch=2,
        grid=(tiles // count,),
        in_specs=[
            pl.BlockSpec((part, width), lambda i, *_: (i, 0)),
            pl.BlockSpec((feats.shape[0], part), lambda i, *_: (0, i)),
            pl.BlockSpec((count, 2, tile, tile), lambda i, *_: (i, 0, 0, 0)),
            pl.BlockSpec((part, dw.shape[1]), lambda i, *_: (i, 0)),
            all_of(halo),
            all_of(local),
            all_of(drv),
            all_of(w1),
            all_of(fw),
            all_of(b1),
            all_of(w2),
            all_of(b2),
        ],
        out_specs=pl.BlockSpec((part, width), lambda i, *_: (i, 0)),
        scratch_shapes=[pltpu.VMEM((part, width), jnp.bfloat16)],
    )
    return pl.pallas_call(
        functools.partial(update_kernel, count),
        grid_spec=grid_spec,
        out_shape=jax.ShapeDtypeStruct((rows, width), jnp.bfloat16),
        compiler_params=pltpu.CompilerParams(vmem_limit_bytes=40 * 1024 * 1024),
        name="update",
    )(keys, halo_slot, embedding, feats, adjacency, dw, halo, local, drv, w1, fw, b1, w2, b2)


def per_device(
    embedding,
    scenario_feats,
    adjacency,
    driver_weight,
    local_slot,
    halo_slot,
    send_rows,
    send_count,
    hot_ids,
    first_weight,
    feature_weight,
    first_bias,
    second_weight,
    second_bias,
):
    n_dom, n_scen = lax.axis_size("dom"), lax.axis_size("scen")
    halo, local, drivers, w1, w2, keys = exchange(
        hot_ids,
        local_slot,
        send_rows,
        send_count,
        embedding,
        first_weight,
        second_weight,
        n_dom,
        n_scen,
        adjacency.shape[-1],
    )
    return update(
        keys,
        halo_slot,
        embedding,
        scenario_feats,
        adjacency,
        driver_weight,
        halo,
        local,
        drivers,
        w1,
        feature_weight,
        first_bias,
        w2,
        second_bias,
    )


def solution(mesh):
    return jax.shard_map(
        per_device,
        mesh=mesh,
        in_specs=(
            P(("dom", "scen"), None),
            P(None, ("dom", "scen")),
            P(("dom", "scen"), None, None, None),
            P(("dom", "scen"), None),
            P(("dom", "scen")),
            P(("dom", "scen")),
            P(("dom", "scen"), None),
            P(("dom", "scen")),
            P(),
            P("scen", None),
            P(),
            P(),
            P("scen", None),
            P(),
        ),
        out_specs=P(("dom", "scen"), None),
        check_vma=False,
    )
```

```python
import functools

import jax
import jax.numpy as jnp
from jax import lax
from jax.experimental import pallas as pl
from jax.experimental.pallas import tpu as pltpu
from jax.sharding import PartitionSpec as P

MESH = pl.DeviceIdType.MESH
LANES = 128
GROUP = 256
PAD = 16


def flipped(index, mask):
    bit = 1
    while bit <= mask:
        if mask & bit:
            index = index + bit * (1 - 2 * ((index // bit) % 2))
        bit *= 2
    return index


def spread(row):
    across = jnp.broadcast_to(row.astype(jnp.float32), (LANES, LANES))
    return across, across.T


def whole_part(values, size):
    return jnp.floor((values + 0.5) * (1.0 / size))


def iota_f32(shape, dim):
    return lax.broadcasted_iota(jnp.int32, shape, dim).astype(jnp.float32)


def picked_rows(column, emb_ref):
    tiles, tile, width = emb_ref.shape
    rows = tiles * tile
    lane = iota_f32(column.shape, 1)
    blocks = [
        jnp.where(column == lane + float(at), 1.0, 0.0).astype(jnp.bfloat16)
        for at in range(0, rows, LANES)
    ]
    return jnp.dot(
        jnp.concatenate(blocks, axis=1),
        emb_ref[...].reshape(rows, width),
        preferred_element_type=jnp.float32,
    ).astype(jnp.bfloat16)


def layer_kernel(
    n_dom,
    n_scen,
    cap,
    hot_hbm,
    slot_hbm,
    halo_slot_hbm,
    rows_hbm,
    count_hbm,
    emb_hbm,
    feats_hbm,
    adj_hbm,
    dw_hbm,
    w1_hbm,
    fw_hbm,
    b1_hbm,
    w2_hbm,
    b2_hbm,
    result_hbm,
    hot_ref,
    slot_ref,
    halo_slot_ref,
    rows_ref,
    count_ref,
    emb_ref,
    feats_ref,
    adj_ref,
    dw_ref,
    fw_ref,
    b1_ref,
    b2_ref,
    w1f_ref,
    w2f_ref,
    halo_ref,
    local_ref,
    drv_ref,
    keys_ref,
    keys_smem,
    out_buf,
    stage,
    myreq,
    reqs,
    reqs_smem,
    mine,
    gat1,
    gat2,
    padrow,
    agg_ref,
    inner_ref,
    result_ref,
    in_sem,
    halo_send,
    halo_recv,
    req_send,
    req_recv,
    loc_send,
    loc_recv,
    d1_send,
    d1_recv,
    d2_send,
    d2_recv,
    w1_send,
    w1_recv,
    w2_send,
    w2_recv,
    own_sem,
    result_sem,
):
    d = lax.axis_index("dom")
    s = lax.axis_index("scen")
    tiles, tile, width = emb_ref.shape
    rows = tiles * tile
    per = tiles // n_scen
    per_group = max(1, GROUP // cap)
    n_groups = n_dom // per_group
    drv_rows = n_dom * PAD

    def dom_peers(body):
        def step(k, carry):
            body(lax.rem(d + k, n_dom))
            return carry

        lax.fori_loop(1, n_dom, step, 0)

    def scen_peers(body):
        for k in range(n_scen - 1, 0, -1):
            body(flipped(s, k))

    def remote(src, dst, send, recv, where):
        return pltpu.make_async_remote_copy(
            src_ref=src,
            dst_ref=dst,
            send_sem=send,
            recv_sem=recv,
            device_id=where,
            device_id_type=MESH,
        )

    def block(ref, index, size):
        return ref.at[pl.ds(pl.multiple_of(index * size, size), size)]

    def halo_place(index):
        if cap >= tile:
            return halo_ref.at[pl.ds(index * (cap // tile), cap // tile)]
        share = tile // cap
        return halo_ref.at[
            index // share, pl.ds(pl.multiple_of((index % share) * cap, cap), cap)
        ]

    def halo_source(index):
        if cap >= tile:
            return out_buf.at[pl.ds(index * (cap // tile), cap // tile)]
        share = tile // cap
        return out_buf.at[
            index // share, pl.ds(pl.multiple_of((index % share) * cap, cap), cap)
        ]

    def halo_copy(peer, mark):
        return remote(
            halo_source(peer),
            halo_place(mark),
            halo_send.at[peer],
            halo_recv.at[mark],
            {"dom": peer},
        )

    def req_copy(peer, mark):
        return remote(myreq, reqs.at[mark], req_send.at[peer], req_recv.at[mark], {"scen": peer})

    def loc_copy(peer, mark):
        return remote(
            stage.at[pl.ds(peer * per, per)],
            local_ref.at[pl.ds(mark * per, per)],
            loc_send.at[peer],
            loc_recv.at[mark],
            {"scen": peer},
        )

    def d1_copy(peer, mark):
        return remote(
            mine, block(gat1, mark, PAD), d1_send.at[peer], d1_recv.at[mark], {"dom": peer}
        )

    def d2_copy(peer, mark):
        return remote(
            gat1, block(gat2, mark, drv_rows), d2_send.at[peer], d2_recv.at[mark], {"scen": peer}
        )

    def w1_copy(peer, mark):
        return remote(
            w1_hbm,
            block(w1f_ref, mark, w1_hbm.shape[0]),
            w1_send.at[peer],
            w1_recv.at[mark],
            {"scen": peer},
        )

    def w2_copy(peer, mark):
        return remote(
            w2_hbm,
            block(w2f_ref, mark, w2_hbm.shape[0]),
            w2_send.at[peer],
            w2_recv.at[mark],
            {"scen": peer},
        )

    loads = {}

    def load(name, src, dst):
        loads[name] = pltpu.make_async_copy(src, dst, in_sem.at[len(loads)])
        loads[name].start()

    load("slot", slot_hbm, slot_ref)
    load("count", count_hbm, count_ref)
    load("rows", rows_hbm, rows_ref)
    load("hot", hot_hbm, hot_ref)
    load("emb", emb_hbm, emb_ref)

    barrier = pltpu.get_barrier_semaphore()
    dom_peers(
        lambda p: pl.semaphore_signal(
            barrier, inc=1, device_id={"dom": p}, device_id_type=MESH
        )
    )
    scen_peers(
        lambda u: pl.semaphore_signal(
            barrier, inc=1, device_id={"scen": u}, device_id_type=MESH
        )
    )

    load("halo_slot", halo_slot_hbm, halo_slot_ref)
    load("w1", w1_hbm, block(w1f_ref, s, w1_hbm.shape[0]))
    load("w2", w2_hbm, block(w2f_ref, s, w2_hbm.shape[0]))
    load("feats", feats_hbm, feats_ref)
    load("fw", fw_hbm, fw_ref)
    load("b1", b1_hbm, b1_ref)
    load("b2", b2_hbm, b2_ref)
    load("dw", dw_hbm, dw_ref)
    load("adj", adj_hbm, adj_ref)

    square = (LANES, LANES)
    lane = iota_f32(square, 1)
    sub = iota_f32(square, 0)

    padrow[...] = jnp.full(padrow.shape, -1, jnp.int32)
    loads["slot"].wait()
    padrow[0:1, 0:tiles] = slot_ref[...]
    across = jnp.broadcast_to(padrow[0:1, :], square)
    down = across.T
    ilane = lax.broadcasted_iota(jnp.int32, square, 1)
    isub = lax.broadcasted_iota(jnp.int32, square, 0)

    def holder(slots):
        found = jnp.where(slots >= 0, 0, -1)
        for u in range(1, n_scen):
            found = found + jnp.where(slots >= u * tiles, 1, 0)
        return found

    own_a, own_d = holder(across), holder(down)
    same = own_a == own_d
    rank_col = jnp.sum(jnp.where(same & (ilane < isub), 1, 0), axis=1, keepdims=True)
    rank_row = jnp.sum(jnp.where(same & (isub < ilane), 1, 0), axis=0, keepdims=True)
    key_col = jnp.where(isub < tiles, own_d * per + rank_col, -1)
    wanted = jnp.sum(
        jnp.where(key_col == ilane, down - own_d * tiles, 0), axis=0, keepdims=True
    )
    myreq[...] = jnp.broadcast_to(wanted, myreq.shape)
    keys_ref[...] = jnp.broadcast_to(own_a[0:1, :] * per + rank_row, keys_ref.shape)

    pl.semaphore_wait(barrier, n_dom - 1 + n_scen - 1)
    scen_peers(lambda u: req_copy(u, s).start())

    for name in ("count", "rows", "hot", "emb"):
        loads[name].wait()

    def row_of(index, columns):
        block_of = rows_ref[:, columns]
        at = lax.broadcasted_iota(jnp.int32, block_of.shape, 0)
        return jnp.sum(jnp.where(at == index, block_of, 0), axis=0, keepdims=True)

    def halo_group(group):
        first = group * per_group
        columns = []
        for half in range(GROUP // LANES):
            if cap >= LANES:
                parts = cap // LANES
                assert per_group == 1 and parts == GROUP // LANES
                row = row_of(first, slice(half * LANES, (half + 1) * LANES))
                limit = count_ref[first]
                place = lax.broadcasted_iota(jnp.int32, (1, LANES), 1) + half * LANES
                row = jnp.where(place < limit, row, -1)
            else:
                parts = LANES // cap
                row = row_of(group * (GROUP // LANES) + half, slice(0, LANES))
                place = lax.broadcasted_iota(jnp.int32, (1, LANES), 1)
                live = place < 0
                for i in range(parts):
                    limit = count_ref[first + half * parts + i]
                    live = live | ((place >= i * cap) & (place < i * cap + limit) & (place < (i + 1) * cap))
                row = jnp.where(live, row, -1)
            columns.append(spread(row)[1])
        out_buf[pl.ds(group * (GROUP // LANES), GROUP // LANES)] = picked_rows(
            jnp.concatenate(columns, axis=0), emb_ref
        ).reshape(GROUP // LANES, LANES, width)

    def halo_start(group):
        halo_group(group)
        if per_group == 1:
            halo_copy(group, d).start()
            return

        def step(i, carry):
            p = group * per_group + i

            @pl.when(p != d)
            def _():
                halo_copy(p, d).start()

            return carry

        lax.fori_loop(0, per_group, step, 0)

    my_group = d // per_group
    half_way = n_groups // 2
    order = []
    for k in range(half_way - 1, 0, -1):
        far, near = flipped(my_group, k + half_way), flipped(my_group, k)
        order.append(far + (near - far) * (s % 2))
        order.append(near + (far - near) * (s % 2))
    order.append(flipped(my_group, half_way))
    halo_start(order[0])

    r_ids, c_ids = spread(hot_ref[...])
    r_own, c_own = whole_part(r_ids, rows), whole_part(c_ids, rows)
    equal = r_ids == c_ids
    new_col = 1.0 - jnp.max(jnp.where(equal & (lane < sub), 1.0, 0.0), axis=1, keepdims=True)
    new_row = 1.0 - jnp.max(jnp.where(equal & (sub < lane), 1.0, 0.0), axis=0, keepdims=True)
    alike = r_own == c_own
    hot_rank_row = jnp.sum(
        jnp.where(alike & (c_ids < r_ids), new_col, 0.0), axis=0, keepdims=True
    )
    hot_rank_col = jnp.sum(
        jnp.where(alike & (r_ids < c_ids), new_row, 0.0), axis=1, keepdims=True
    )
    me = (d * n_scen + s).astype(jnp.float32)
    own_rows = picked_rows(c_ids - me * float(rows), emb_ref)
    chosen = jnp.where(
        (iota_f32((PAD, LANES), 0) == hot_rank_row) & (r_own[0:1, :] == me), new_row, 0.0
    ).astype(jnp.bfloat16)
    mine[...] = jnp.dot(chosen, own_rows, preferred_element_type=jnp.float32).astype(jnp.bfloat16)
    block(gat1, d, PAD)[...] = mine[...]
    dom_peers(lambda p: d1_copy(p, d).start())

    halo_start(order[1])

    scen_peers(lambda u: req_copy(u, u).wait_recv())
    reqs[pl.ds(s, 1)] = myreq[...][None]
    fetch = pltpu.make_async_copy(reqs, reqs_smem, own_sem.at[0])
    fetch.start()
    fetch.wait()

    def stage_for(u):
        for r in range(per):
            slot = reqs_smem[u, 0, s * per + r]
            stage[pl.ds(u * per + r, 1)] = emb_ref[slot][None]

    def serve(u):
        stage_for(u)
        loc_copy(u, s).start()

    scen_peers(serve)
    scen_peers(lambda u: w1_copy(u, s).start())
    scen_peers(lambda u: w2_copy(u, s).start())
    stage_for(s)
    local_ref[pl.ds(s * per, per)] = stage[pl.ds(s * per, per)]

    for group in order[2:]:
        halo_start(group)
    if per_group == 1:
        halo_group(my_group)
    else:
        halo_start(my_group)
    halo_place(d)[...] = halo_source(d)[...]

    dom_peers(lambda p: d1_copy(p, p).wait_recv())
    scen_peers(lambda u: d2_copy(u, s).start())
    block(gat2, s, drv_rows)[...] = gat1[...]
    scen_peers(lambda u: d2_copy(u, u).wait_recv())
    c_dom = whole_part(c_own, n_scen)
    place = (c_own - c_dom * float(n_scen)) * float(drv_rows) + c_dom * float(PAD) + hot_rank_col
    total = jnp.zeros(drv_ref.shape, jnp.float32)
    for at in range(0, n_scen * drv_rows, LANES):
        pick = jnp.where(place == lane + float(at), 1.0, 0.0).astype(jnp.bfloat16)
        total += jnp.dot(pick, gat2[at : at + LANES, :], preferred_element_type=jnp.float32)
    drv_ref[...] = total.astype(jnp.bfloat16)


    for name in ("feats", "fw", "b1", "w1", "w2", "b2", "dw", "adj", "halo_slot"):
        loads[name].wait()
    scen_peers(lambda u: w1_copy(u, u).wait())
    scen_peers(lambda u: w2_copy(u, u).wait())
    count = 4 if tiles % 4 == 0 else 1
    part = count * tile

    def own_part(i, carry):
        here = pl.ds(pl.multiple_of(i * part, part), part)
        inner = jnp.dot(
            emb_ref[pl.ds(i * count, count)].reshape(part, width),
            w1f_ref[:width, :],
            preferred_element_type=jnp.float32,
        )
        inner += lax.dot_general(
            feats_ref[:, here],
            fw_ref[...],
            (((0,), (0,)), ((), ())),
            preferred_element_type=jnp.float32,
        )
        inner_ref[here, :] = inner + b1_ref[...]
        return carry

    lax.fori_loop(0, tiles // count, own_part, 0)

    scen_peers(lambda u: loc_copy(u, u).wait())
    keys_copy = pltpu.make_async_copy(keys_ref, keys_smem, own_sem.at[1])
    keys_copy.start()
    keys_copy.wait()

    def local_part(i, carry):
        weights = jnp.concatenate([adj_ref[i, 0], dw_ref[i]], axis=1)
        sources = jnp.concatenate([local_ref[keys_smem[0, i]], drv_ref[...]], axis=0)
        agg_ref[i] = jnp.dot(weights, sources, preferred_element_type=jnp.float32)
        return carry

    lax.fori_loop(0, tiles, local_part, 0)

    dom_peers(lambda p: d1_copy(p, p).wait_send())
    for make in (req_copy, d2_copy):
        scen_peers(lambda u: make(u, u).wait_send())
    dom_peers(lambda p: halo_copy(p, p).wait())

    def result_copy(i):
        here = pl.ds(pl.multiple_of(i * part, part), part)
        return pltpu.make_async_copy(
            result_ref.at[here], result_hbm.at[here], result_sem.at[i]
        )

    def last_part(i, carry):
        here = pl.ds(pl.multiple_of(i * part, part), part)
        totals = []
        for j in range(count):
            t = i * count + j
            total = agg_ref[t] + jnp.dot(
                adj_ref[t, 1], halo_ref[halo_slot_ref[t]], preferred_element_type=jnp.float32
            )
            totals.append(total.astype(jnp.bfloat16))
        inner = inner_ref[here, :] + jnp.dot(
            jnp.concatenate(totals, axis=0),
            w1f_ref[width:, :],
            preferred_element_type=jnp.float32,
        )
        activated = (0.5 * inner * (1.0 + lax.erf(inner * (0.5**0.5)))).astype(jnp.bfloat16)
        result = jnp.dot(activated, w2f_ref[...], preferred_element_type=jnp.float32)
        own = emb_ref[pl.ds(i * count, count)].reshape(part, width).astype(jnp.float32)
        result_ref[here, :] = (result + (own + b2_ref[...])).astype(jnp.bfloat16)
        result_copy(i).start()
        return carry

    lax.fori_loop(0, tiles // count, last_part, 0)

    def finish(i, carry):
        result_copy(i).wait()
        return carry

    lax.fori_loop(0, tiles // count, finish, 0)


def per_device(
    embedding,
    scenario_feats,
    adjacency,
    driver_weight,
    local_slot,
    halo_slot,
    send_rows,
    send_count,
    hot_ids,
    first_weight,
    feature_weight,
    first_bias,
    second_weight,
    second_bias,
):
    n_dom, n_scen = lax.axis_size("dom"), lax.axis_size("scen")
    rows, width = embedding.shape
    tiles, _, tile, _ = adjacency.shape
    slots, cap = send_rows.size, send_rows.shape[1]
    hot = hot_ids.shape[0]
    assert -(-hot // (n_dom * n_scen)) <= PAD and tile == LANES
    if cap < LANES:
        send_rows = send_rows.reshape(-1, LANES)
    bf16, f32, i32 = jnp.bfloat16, jnp.float32, jnp.int32
    vmem, smem, dma = pltpu.VMEM, pltpu.SMEM, pltpu.SemaphoreType.DMA
    anywhere = pl.BlockSpec(memory_space=pl.ANY)
    operands = (
        hot_ids.reshape(1, -1),
        local_slot.reshape(1, -1),
        halo_slot,
        send_rows,
        send_count,
        embedding.reshape(tiles, tile, width),
        scenario_feats,
        adjacency,
        driver_weight.reshape(tiles, tile, hot),
        first_weight,
        feature_weight,
        first_bias.reshape(1, -1),
        second_weight,
        second_bias.reshape(1, -1),
    )
    by_dom = [dma((n_dom,)), dma((n_dom,))]
    by_scen = [dma((n_scen,)), dma((n_scen,))]
    return pl.pallas_call(
        functools.partial(layer_kernel, n_dom, n_scen, cap),
        out_shape=jax.ShapeDtypeStruct((rows, width), bf16),
        in_specs=[anywhere] * len(operands),
        out_specs=anywhere,
        scratch_shapes=[
            vmem((1, hot), i32),
            vmem((1, tiles), i32),
            smem(halo_slot.shape, i32),
            vmem(send_rows.shape, i32),
            smem(send_count.shape, i32),
            vmem((tiles, tile, width), bf16),
            vmem(scenario_feats.shape, bf16),
            vmem(adjacency.shape, bf16),
            vmem((tiles, tile, hot), bf16),
            vmem(feature_weight.shape, bf16),
            vmem((1, width), f32),
            vmem((1, width), f32),
            vmem((n_scen * first_weight.shape[0], width), bf16),
            vmem((n_scen * second_weight.shape[0], width), bf16),
            vmem((slots // tile, tile, width), bf16),
            vmem((tiles, tile, width), bf16),
            vmem((hot, width), bf16),
            vmem((8, LANES), i32),
            smem((8, LANES), i32),
            vmem((slots // tile, tile, width), bf16),
            vmem((tiles, tile, width), bf16),
            vmem((8, LANES), i32),
            vmem((n_scen, 8, LANES), i32),
            smem((n_scen, 8, LANES), i32),
            vmem((PAD, width), bf16),
            vmem((n_dom * PAD, width), bf16),
            vmem((n_scen * n_dom * PAD, width), bf16),
            vmem((8, LANES), i32),
            vmem((tiles, tile, width), f32),
            vmem((rows, width), f32),
            vmem((rows, width), bf16),
            dma((len(operands),)),
            *by_dom,
            *by_scen,
            *by_scen,
            *by_dom,
            *by_scen,
            *by_scen,
            *by_scen,
            dma((2,)),
            dma((tiles,)),
        ],
        compiler_params=pltpu.CompilerParams(
            collective_id=0, has_side_effects=True, vmem_limit_bytes=60 * 1024 * 1024
        ),
        name="layer",
    )(*operands)


def solution(mesh):
    return jax.shard_map(
        per_device,
        mesh=mesh,
        in_specs=(
            P(("dom", "scen"), None),
            P(None, ("dom", "scen")),
            P(("dom", "scen"), None, None, None),
            P(("dom", "scen"), None),
            P(("dom", "scen")),
            P(("dom", "scen")),
            P(("dom", "scen"), None),
            P(("dom", "scen")),
            P(),
            P("scen", None),
            P(),
            P(),
            P("scen", None),
            P(),
        ),
        out_specs=P(("dom", "scen"), None),
        check_vma=False,
    )
```

```python
import functools

import jax
import jax.numpy as jnp
from jax import lax
from jax.experimental import pallas as pl
from jax.experimental.pallas import tpu as pltpu
from jax.sharding import PartitionSpec as P

MESH = pl.DeviceIdType.MESH
LANES = 128
GROUP = 256
PAD = 16


def flipped(index, mask):
    bit = 1
    while bit <= mask:
        if mask & bit:
            index = index + bit * (1 - 2 * ((index // bit) % 2))
        bit *= 2
    return index


def spread(row):
    across = jnp.broadcast_to(row.astype(jnp.float32), (LANES, LANES))
    return across, across.T


def whole_part(values, size):
    return jnp.floor((values + 0.5) * (1.0 / size))


def iota_f32(shape, dim):
    return lax.broadcasted_iota(jnp.int32, shape, dim).astype(jnp.float32)


def picked_rows(column, emb_ref):
    tiles, tile, width = emb_ref.shape
    rows = tiles * tile
    lane = iota_f32(column.shape, 1)
    blocks = [
        jnp.where(column == lane + float(at), 1.0, 0.0).astype(jnp.bfloat16)
        for at in range(0, rows, LANES)
    ]
    return jnp.dot(
        jnp.concatenate(blocks, axis=1),
        emb_ref[...].reshape(rows, width),
        preferred_element_type=jnp.float32,
    ).astype(jnp.bfloat16)


def gather_kernel(
    n_dom,
    n_scen,
    cap,
    hot_cap,
    hot_hbm,
    slot_hbm,
    rows_hbm,
    count_hbm,
    emb_hbm,
    feats_hbm,
    adj_hbm,
    dw_hbm,
    w1_hbm,
    fw_hbm,
    b1_hbm,
    w2_hbm,
    halo_ref,
    inner_hbm,
    w1b_hbm,
    w2f_hbm,
    hot_ref,
    slot_ref,
    rows_ref,
    count_ref,
    emb_ref,
    feats_ref,
    adj_ref,
    dw_ref,
    fw_ref,
    b1_ref,
    w1f_ref,
    w2f_ref,
    local_ref,
    drv_ref,
    keys_ref,
    keys_smem,
    out_buf,
    stage,
    myreq,
    reqs,
    reqs_smem,
    mine,
    gat1,
    gat2,
    padrow,
    inner_ref,
    in_sem,
    halo_send,
    halo_recv,
    req_send,
    req_recv,
    loc_send,
    loc_recv,
    d1_send,
    d1_recv,
    d2_send,
    d2_recv,
    w1_send,
    w1_recv,
    w2_send,
    w2_recv,
    own_sem,
    inner_sem,
):
    d = lax.axis_index("dom")
    s = lax.axis_index("scen")
    tiles, tile, width = emb_ref.shape
    rows = tiles * tile
    per = tiles // n_scen
    per_group = max(1, GROUP // cap)
    n_groups = n_dom // per_group
    drv_rows = n_dom * hot_cap

    def dom_peers(body):
        def step(k, carry):
            body(lax.rem(d + k, n_dom))
            return carry

        lax.fori_loop(1, n_dom, step, 0)

    def scen_peers(body):
        for k in range(n_scen - 1, 0, -1):
            body(flipped(s, k))

    def remote(src, dst, send, recv, where):
        return pltpu.make_async_remote_copy(
            src_ref=src,
            dst_ref=dst,
            send_sem=send,
            recv_sem=recv,
            device_id=where,
            device_id_type=MESH,
        )

    def block(ref, index, size):
        return ref.at[pl.ds(pl.multiple_of(index * size, size), size)]

    def halo_place(index):
        if cap >= tile:
            return halo_ref.at[pl.ds(index * (cap // tile), cap // tile)]
        share = tile // cap
        return halo_ref.at[
            index // share, pl.ds(pl.multiple_of((index % share) * cap, cap), cap)
        ]

    def halo_source(index):
        if cap >= tile:
            return out_buf.at[pl.ds(index * (cap // tile), cap // tile)]
        share = tile // cap
        return out_buf.at[
            index // share, pl.ds(pl.multiple_of((index % share) * cap, cap), cap)
        ]

    def halo_copy(peer, mark):
        return remote(
            halo_source(peer),
            halo_place(mark),
            halo_send.at[peer],
            halo_recv.at[mark],
            {"dom": peer},
        )

    def req_copy(peer, mark):
        return remote(myreq, reqs.at[mark], req_send.at[peer], req_recv.at[mark], {"scen": peer})

    def loc_copy(peer, mark):
        return remote(
            stage.at[pl.ds(peer * per, per)],
            local_ref.at[pl.ds(mark * per, per)],
            loc_send.at[peer],
            loc_recv.at[mark],
            {"scen": peer},
        )

    def d1_copy(peer, mark):
        return remote(
            mine, block(gat1, mark, PAD), d1_send.at[peer], d1_recv.at[mark], {"dom": peer}
        )

    doubling = []
    held, mask = [0], n_scen // 2
    while mask:
        doubling.append([(mask, k) for k in held])
        held, mask = held + [k + mask for k in held], mask // 2

    def doubled(ref, send, recv, mask, k):
        part = block(ref, flipped(s, k), ref.shape[0] // n_scen)
        at = (n_scen // (2 * mask) - 1) + held.index(k)
        return remote(part, part, send.at[at], recv.at[at], {"scen": flipped(s, mask)})

    def arriving(ref, send, recv, mask, k):
        part = block(ref, flipped(s, k + mask), ref.shape[0] // n_scen)
        at = (n_scen // (2 * mask) - 1) + held.index(k)
        return remote(part, part, send.at[at], recv.at[at], {"scen": flipped(s, mask)})

    both_weights = ((w1f_ref, w1_send, w1_recv), (w2f_ref, w2_send, w2_recv))
    drivers = ((gat2, d2_send, d2_recv),)

    def start_step(arrays, step):
        for mask, k in doubling[step]:
            for array in arrays:
                doubled(*array, mask, k).start()

    def wait_step(arrays, step):
        for mask, k in doubling[step]:
            for array in arrays:
                arriving(*array, mask, k).wait_recv()

    def sent(arrays):
        for steps in doubling:
            for mask, k in steps:
                for array in arrays:
                    doubled(*array, mask, k).wait_send()

    loads = {}

    def load(name, src, dst):
        loads[name] = pltpu.make_async_copy(src, dst, in_sem.at[len(loads)])
        loads[name].start()

    load("slot", slot_hbm, slot_ref)
    load("w1", w1_hbm, block(w1f_ref, s, w1_hbm.shape[0]))
    load("w2", w2_hbm, block(w2f_ref, s, w2_hbm.shape[0]))
    load("count", count_hbm, count_ref)
    load("rows", rows_hbm, rows_ref)
    load("hot", hot_hbm, hot_ref)
    quarter = tiles // 4
    for i in range(4):
        piece = pl.ds(i * quarter, quarter)
        load(f"emb{i}", emb_hbm.at[piece], emb_ref.at[piece])

    barrier = pltpu.get_barrier_semaphore()
    dom_peers(
        lambda p: pl.semaphore_signal(
            barrier, inc=1, device_id={"dom": p}, device_id_type=MESH
        )
    )
    scen_peers(
        lambda u: pl.semaphore_signal(
            barrier, inc=1, device_id={"scen": u}, device_id_type=MESH
        )
    )

    load("feats", feats_hbm, feats_ref)
    load("fw", fw_hbm, fw_ref)
    load("b1", b1_hbm, b1_ref)
    load("dw", dw_hbm, dw_ref)
    load("adj", adj_hbm, adj_ref)

    square = (LANES, LANES)
    lane = iota_f32(square, 1)
    sub = iota_f32(square, 0)

    padrow[...] = jnp.full(padrow.shape, -1, jnp.int32)
    loads["slot"].wait()
    padrow[0:1, 0:tiles] = slot_ref[...]
    across = jnp.broadcast_to(padrow[0:1, :], square)
    down = across.T
    ilane = lax.broadcasted_iota(jnp.int32, square, 1)
    isub = lax.broadcasted_iota(jnp.int32, square, 0)

    def holder(slots):
        found = jnp.where(slots >= 0, 0, -1)
        for u in range(1, n_scen):
            found = found + jnp.where(slots >= u * tiles, 1, 0)
        return found

    own_a, own_d = holder(across), holder(down)
    same = own_a == own_d
    rank_col = jnp.sum(jnp.where(same & (ilane < isub), 1, 0), axis=1, keepdims=True)
    rank_row = jnp.sum(jnp.where(same & (isub < ilane), 1, 0), axis=0, keepdims=True)
    key_col = jnp.where(isub < tiles, own_d * per + rank_col, -1)
    wanted = jnp.sum(
        jnp.where(key_col == ilane, down - own_d * tiles, 0), axis=0, keepdims=True
    )
    myreq[...] = jnp.broadcast_to(wanted, myreq.shape)
    keys_ref[...] = jnp.broadcast_to(own_a[0:1, :] * per + rank_row, keys_ref.shape)

    pl.semaphore_wait(barrier, n_dom - 1 + n_scen - 1)
    scen_peers(lambda u: req_copy(u, s).start())
    loads["w1"].wait()
    loads["w2"].wait()
    start_step(both_weights, 0)

    for name in ("count", "rows", "hot", "emb0", "emb1", "emb2", "emb3"):
        loads[name].wait()

    def row_of(index, columns):
        block_of = rows_ref[:, columns]
        at = lax.broadcasted_iota(jnp.int32, block_of.shape, 0)
        return jnp.sum(jnp.where(at == index, block_of, 0), axis=0, keepdims=True)

    def halo_group(group):
        first = group * per_group
        columns = []
        for half in range(GROUP // LANES):
            if cap >= LANES:
                parts = cap // LANES
                assert per_group == 1 and parts == GROUP // LANES
                row = row_of(first, slice(half * LANES, (half + 1) * LANES))
                limit = count_ref[first]
                place = lax.broadcasted_iota(jnp.int32, (1, LANES), 1) + half * LANES
                row = jnp.where(place < limit, row, -1)
            else:
                parts = LANES // cap
                row = row_of(group * (GROUP // LANES) + half, slice(0, LANES))
                place = lax.broadcasted_iota(jnp.int32, (1, LANES), 1)
                live = place < 0
                for i in range(parts):
                    limit = count_ref[first + half * parts + i]
                    live = live | ((place >= i * cap) & (place < i * cap + limit) & (place < (i + 1) * cap))
                row = jnp.where(live, row, -1)
            columns.append(spread(row)[1])
        out_buf[pl.ds(group * (GROUP // LANES), GROUP // LANES)] = picked_rows(
            jnp.concatenate(columns, axis=0), emb_ref
        ).reshape(GROUP // LANES, LANES, width)

    def halo_start(group):
        halo_group(group)
        if per_group == 1:
            halo_copy(group, d).start()
            return

        def step(i, carry):
            p = group * per_group + i

            @pl.when(p != d)
            def _():
                halo_copy(p, d).start()

            return carry

        lax.fori_loop(0, per_group, step, 0)

    my_group = d // per_group
    half_way = n_groups // 2
    order = []
    for k in range(half_way - 1, 0, -1):
        far, near = flipped(my_group, k + half_way), flipped(my_group, k)
        order.append(far + (near - far) * (s % 2))
        order.append(near + (far - near) * (s % 2))
    order.append(flipped(my_group, half_way))
    halo_start(order[0])

    scen_peers(lambda u: req_copy(u, u).wait_recv())
    reqs[pl.ds(s, 1)] = myreq[...][None]
    fetch = pltpu.make_async_copy(reqs, reqs_smem, own_sem.at[0])
    fetch.start()
    fetch.wait()

    def stage_for(u):
        for r in range(per):
            slot = reqs_smem[u, 0, s * per + r]
            stage[pl.ds(u * per + r, 1)] = emb_ref[slot][None]

    def serve(u):
        stage_for(u)
        loc_copy(u, s).start()

    scen_peers(serve)
    stage_for(s)
    local_ref[pl.ds(s * per, per)] = stage[pl.ds(s * per, per)]

    halo_start(order[1])

    r_ids, c_ids = spread(hot_ref[...])
    r_own, c_own = whole_part(r_ids, rows), whole_part(c_ids, rows)
    equal = r_ids == c_ids
    new_col = 1.0 - jnp.max(jnp.where(equal & (lane < sub), 1.0, 0.0), axis=1, keepdims=True)
    new_row = 1.0 - jnp.max(jnp.where(equal & (sub < lane), 1.0, 0.0), axis=0, keepdims=True)
    alike = r_own == c_own
    hot_rank_row = jnp.sum(
        jnp.where(alike & (c_ids < r_ids), new_col, 0.0), axis=0, keepdims=True
    )
    hot_rank_col = jnp.sum(
        jnp.where(alike & (r_ids < c_ids), new_row, 0.0), axis=1, keepdims=True
    )
    me = (d * n_scen + s).astype(jnp.float32)
    own_rows = picked_rows(c_ids - me * float(rows), emb_ref)
    chosen = jnp.where(
        (iota_f32((PAD, LANES), 0) == hot_rank_row) & (r_own[0:1, :] == me), new_row, 0.0
    ).astype(jnp.bfloat16)
    mine[...] = jnp.dot(chosen, own_rows, preferred_element_type=jnp.float32).astype(jnp.bfloat16)
    block(gat1, d, PAD)[...] = mine[...]
    dom_peers(lambda p: d1_copy(p, d).start())

    for group in order[2:]:
        halo_start(group)
    if per_group == 1:
        halo_group(my_group)
    else:
        halo_start(my_group)
    own_halo = pltpu.make_async_copy(halo_source(d), halo_place(d), own_sem.at[2])
    own_halo.start()

    wait_step(both_weights, 0)
    start_step(both_weights, 1)

    dom_peers(lambda p: d1_copy(p, p).wait_recv())
    at_row = iota_f32((drv_rows, n_dom * PAD), 0)
    at_dom = whole_part(at_row, hot_cap)
    keep = at_dom * float(PAD) + (at_row - at_dom * float(hot_cap))
    keep = jnp.where(keep == iota_f32(keep.shape, 1), 1.0, 0.0).astype(jnp.bfloat16)
    block(gat2, s, drv_rows)[...] = jnp.dot(
        keep, gat1[...], preferred_element_type=jnp.float32
    ).astype(jnp.bfloat16)
    for step in range(len(doubling)):
        start_step(drivers, step)
        wait_step(drivers, step)
    for step in range(1, len(doubling)):
        wait_step(both_weights, step)
        if step + 1 < len(doubling):
            start_step(both_weights, step + 1)
    c_dom = whole_part(c_own, n_scen)
    place = (c_own - c_dom * float(n_scen)) * float(drv_rows) + c_dom * float(hot_cap) + hot_rank_col
    total = jnp.zeros(drv_ref.shape, jnp.float32)
    for at in range(0, n_scen * drv_rows, LANES):
        pick = jnp.where(place == lane + float(at), 1.0, 0.0).astype(jnp.bfloat16)
        total += jnp.dot(pick, gat2[at : at + LANES, :], preferred_element_type=jnp.float32)
    drv_ref[...] = total.astype(jnp.bfloat16)


    for name in ("feats", "fw", "b1", "dw", "adj"):
        loads[name].wait()
    scen_peers(lambda u: loc_copy(u, u).wait())
    to_out = [
        pltpu.make_async_copy(w1f_ref.at[pl.ds(width, width)], w1b_hbm, own_sem.at[3]),
        pltpu.make_async_copy(w2f_ref, w2f_hbm, own_sem.at[4]),
    ]
    for copy in to_out:
        copy.start()
    keys_copy = pltpu.make_async_copy(keys_ref, keys_smem, own_sem.at[1])
    keys_copy.start()
    keys_copy.wait()
    count = 4 if tiles % 4 == 0 else 1
    part = count * tile

    def inner_copy(i):
        here = pl.ds(pl.multiple_of(i * part, part), part)
        return pltpu.make_async_copy(inner_ref.at[here], inner_hbm.at[here], inner_sem.at[i])

    def own_part(i, carry):
        here = pl.ds(pl.multiple_of(i * part, part), part)
        inner = jnp.dot(
            emb_ref[pl.ds(i * count, count)].reshape(part, width),
            w1f_ref[:width, :],
            preferred_element_type=jnp.float32,
        )
        inner += lax.dot_general(
            feats_ref[:, here],
            fw_ref[...],
            (((0,), (0,)), ((), ())),
            preferred_element_type=jnp.float32,
        )
        totals = []
        for j in range(count):
            t = i * count + j
            weights = jnp.concatenate([adj_ref[t, 0], dw_ref[t]], axis=1)
            sources = jnp.concatenate([local_ref[keys_smem[0, t]], drv_ref[...]], axis=0)
            total = jnp.dot(weights, sources, preferred_element_type=jnp.float32)
            totals.append(total.astype(jnp.bfloat16))
        inner += jnp.dot(
            jnp.concatenate(totals, axis=0),
            w1f_ref[width:, :],
            preferred_element_type=jnp.float32,
        )
        inner_ref[here, :] = inner + b1_ref[...]
        inner_copy(i).start()
        return carry

    lax.fori_loop(0, tiles // count, own_part, 0)

    dom_peers(lambda p: d1_copy(p, p).wait_send())
    scen_peers(lambda u: req_copy(u, u).wait_send())
    sent(both_weights)
    sent(drivers)
    own_halo.wait()
    for copy in to_out:
        copy.wait()

    def finish(i, carry):
        inner_copy(i).wait()
        return carry

    lax.fori_loop(0, tiles // count, finish, 0)
    dom_peers(lambda p: halo_copy(p, p).wait())


def update_kernel(
    count, slot_ref, emb_ref, adj_ref, inner_ref, halo_ref, w1b_ref, w2_ref, b2_ref, out_ref
):
    step = pl.program_id(0)
    totals = []
    for j in range(count):
        halo = halo_ref[slot_ref[step * count + j]]
        total = jnp.dot(adj_ref[j, 0], halo, preferred_element_type=jnp.float32)
        totals.append(total.astype(jnp.bfloat16))
    inner = inner_ref[...] + jnp.dot(
        jnp.concatenate(totals, axis=0), w1b_ref[...], preferred_element_type=jnp.float32
    )
    activated = (0.5 * inner * (1.0 + lax.erf(inner * (0.5**0.5)))).astype(jnp.bfloat16)
    result = jnp.dot(activated, w2_ref[...], preferred_element_type=jnp.float32)
    out_ref[...] = (result + (emb_ref[...].astype(jnp.float32) + b2_ref[...])).astype(
        jnp.bfloat16
    )


def update(halo_slot, embedding, adjacency, inner, halo, w1b, w2, b2):
    rows, width = embedding.shape
    tiles, _, tile, _ = adjacency.shape
    count = 4 if tiles % 4 == 0 else 1
    part = count * tile

    def all_of(array):
        return pl.BlockSpec(array.shape, lambda i, *_: (0,) * array.ndim)

    return pl.pallas_call(
        functools.partial(update_kernel, count),
        grid_spec=pltpu.PrefetchScalarGridSpec(
            num_scalar_prefetch=1,
            grid=(tiles // count,),
            in_specs=[
                pl.BlockSpec((part, width), lambda i, *_: (i, 0)),
                pl.BlockSpec((count, 1, tile, tile), lambda i, *_: (i, 1, 0, 0)),
                pl.BlockSpec((part, width), lambda i, *_: (i, 0)),
                all_of(halo),
                all_of(w1b),
                all_of(w2),
                all_of(b2),
            ],
            out_specs=pl.BlockSpec((part, width), lambda i, *_: (i, 0)),
        ),
        out_shape=jax.ShapeDtypeStruct((rows, width), jnp.bfloat16),
        compiler_params=pltpu.CompilerParams(vmem_limit_bytes=60 * 1024 * 1024),
        name="update",
    )(halo_slot, embedding, adjacency, inner, halo, w1b, w2, b2)


def per_device(
    embedding,
    scenario_feats,
    adjacency,
    driver_weight,
    local_slot,
    halo_slot,
    send_rows,
    send_count,
    hot_ids,
    first_weight,
    feature_weight,
    first_bias,
    second_weight,
    second_bias,
):
    n_dom, n_scen = lax.axis_size("dom"), lax.axis_size("scen")
    rows, width = embedding.shape
    tiles, _, tile, _ = adjacency.shape
    slots, cap = send_rows.size, send_rows.shape[1]
    hot = hot_ids.shape[0]
    hot_cap = -(-hot // (n_dom * n_scen))
    assert hot_cap <= PAD and tile == LANES
    if cap < LANES:
        send_rows = send_rows.reshape(-1, LANES)
    bf16, f32, i32 = jnp.bfloat16, jnp.float32, jnp.int32
    vmem, smem, dma = pltpu.VMEM, pltpu.SMEM, pltpu.SemaphoreType.DMA
    anywhere = pl.BlockSpec(memory_space=pl.ANY)
    operands = (
        hot_ids.reshape(1, -1),
        local_slot.reshape(1, -1),
        send_rows,
        send_count,
        embedding.reshape(tiles, tile, width),
        scenario_feats,
        adjacency,
        driver_weight.reshape(tiles, tile, hot),
        first_weight,
        feature_weight,
        first_bias.reshape(1, -1),
        second_weight,
    )
    by_dom = [dma((n_dom,)), dma((n_dom,))]
    by_scen = [dma((n_scen,)), dma((n_scen,))]
    halo, inner, w1b, w2 = pl.pallas_call(
        functools.partial(gather_kernel, n_dom, n_scen, cap, hot_cap),
        out_shape=(
            jax.ShapeDtypeStruct((slots // tile, tile, width), bf16),
            jax.ShapeDtypeStruct((rows, width), f32),
            jax.ShapeDtypeStruct((width, width), bf16),
            jax.ShapeDtypeStruct((width, width), bf16),
        ),
        in_specs=[anywhere] * len(operands),
        out_specs=(anywhere,) * 4,
        scratch_shapes=[
            vmem((1, hot), i32),
            vmem((1, tiles), i32),
            vmem(send_rows.shape, i32),
            smem(send_count.shape, i32),
            vmem((tiles, tile, width), bf16),
            vmem(scenario_feats.shape, bf16),
            vmem(adjacency.shape, bf16),
            vmem((tiles, tile, hot), bf16),
            vmem(feature_weight.shape, bf16),
            vmem((1, width), f32),
            vmem((n_scen * first_weight.shape[0], width), bf16),
            vmem((n_scen * second_weight.shape[0], width), bf16),
            vmem((tiles, tile, width), bf16),
            vmem((hot, width), bf16),
            vmem((8, LANES), i32),
            smem((8, LANES), i32),
            vmem((slots // tile, tile, width), bf16),
            vmem((tiles, tile, width), bf16),
            vmem((8, LANES), i32),
            vmem((n_scen, 8, LANES), i32),
            smem((n_scen, 8, LANES), i32),
            vmem((PAD, width), bf16),
            vmem((n_dom * PAD, width), bf16),
            vmem((n_scen * n_dom * hot_cap, width), bf16),
            vmem((8, LANES), i32),
            vmem((rows, width), f32),
            dma((len(operands) + 3,)),
            *by_dom,
            *by_scen,
            *by_scen,
            *by_dom,
            *by_scen,
            *by_scen,
            *by_scen,
            dma((5,)),
            dma((tiles,)),
        ],
        compiler_params=pltpu.CompilerParams(
            collective_id=0, has_side_effects=True, vmem_limit_bytes=60 * 1024 * 1024
        ),
        name="gather",
    )(*operands)
    return update(
        halo_slot, embedding, adjacency, inner, halo, w1b, w2, second_bias.reshape(1, -1)
    )


def solution(mesh):
    return jax.shard_map(
        per_device,
        mesh=mesh,
        in_specs=(
            P(("dom", "scen"), None),
            P(None, ("dom", "scen")),
            P(("dom", "scen"), None, None, None),
            P(("dom", "scen"), None),
            P(("dom", "scen")),
            P(("dom", "scen")),
            P(("dom", "scen"), None),
            P(("dom", "scen")),
            P(),
            P("scen", None),
            P(),
            P(),
            P("scen", None),
            P(),
        ),
        out_specs=P(("dom", "scen"), None),
        check_vma=False,
    )
```

```python
import functools

import jax
import jax.numpy as jnp
from jax import lax
from jax.experimental import pallas as pl
from jax.experimental.pallas import tpu as pltpu
from jax.sharding import PartitionSpec as P

MESH = pl.DeviceIdType.MESH
LANES = 128
GROUP = 256
PAD = 16


def flipped(index, mask):
    bit = 1
    while bit <= mask:
        if mask & bit:
            index = index + bit * (1 - 2 * ((index // bit) % 2))
        bit *= 2
    return index


def spread(row):
    across = jnp.broadcast_to(row.astype(jnp.float32), (LANES, LANES))
    return across, across.T


def whole_part(values, size):
    return jnp.floor((values + 0.5) * (1.0 / size))


def iota_f32(shape, dim):
    return lax.broadcasted_iota(jnp.int32, shape, dim).astype(jnp.float32)


def picked_rows(column, emb_ref):
    tiles, tile, width = emb_ref.shape
    rows = tiles * tile
    lane = iota_f32(column.shape, 1)
    blocks = [
        jnp.where(column == lane + float(at), 1.0, 0.0).astype(jnp.bfloat16)
        for at in range(0, rows, LANES)
    ]
    return jnp.dot(
        jnp.concatenate(blocks, axis=1),
        emb_ref[...].reshape(rows, width),
        preferred_element_type=jnp.float32,
    ).astype(jnp.bfloat16)


def gather_kernel(
    n_dom,
    n_scen,
    cap,
    hot_cap,
    hot_hbm,
    slot_hbm,
    rows_hbm,
    count_hbm,
    emb_hbm,
    feats_hbm,
    adj_hbm,
    dw_hbm,
    w1_hbm,
    fw_hbm,
    b1_hbm,
    w2_hbm,
    halo_ref,
    inner_hbm,
    w1b_hbm,
    w2f_hbm,
    hot_ref,
    slot_ref,
    rows_ref,
    count_ref,
    emb_ref,
    feats_ref,
    adj_ref,
    dw_ref,
    fw_ref,
    b1_ref,
    w1f_ref,
    w2f_ref,
    local_ref,
    drv_ref,
    keys_ref,
    keys_smem,
    out_buf,
    stage,
    myreq,
    reqs,
    reqs_smem,
    mine,
    gat1,
    gat2,
    padrow,
    inner_ref,
    in_sem,
    halo_send,
    halo_recv,
    req_send,
    req_recv,
    loc_send,
    loc_recv,
    d1_send,
    d1_recv,
    d2_send,
    d2_recv,
    w1_send,
    w1_recv,
    w2_send,
    w2_recv,
    own_sem,
    inner_sem,
):
    d = lax.axis_index("dom")
    s = lax.axis_index("scen")
    tiles, tile, width = emb_ref.shape
    rows = tiles * tile
    per = tiles // n_scen
    per_group = max(1, GROUP // cap)
    n_groups = n_dom // per_group
    drv_rows = n_dom * hot_cap

    def dom_peers(body):
        def step(k, carry):
            body(lax.rem(d + k, n_dom))
            return carry

        lax.fori_loop(1, n_dom, step, 0)

    def scen_peers(body):
        for k in range(n_scen - 1, 0, -1):
            body(flipped(s, k))

    def remote(src, dst, send, recv, where):
        return pltpu.make_async_remote_copy(
            src_ref=src,
            dst_ref=dst,
            send_sem=send,
            recv_sem=recv,
            device_id=where,
            device_id_type=MESH,
        )

    def block(ref, index, size):
        return ref.at[pl.ds(pl.multiple_of(index * size, size), size)]

    def halo_place(index):
        if cap >= tile:
            return halo_ref.at[pl.ds(index * (cap // tile), cap // tile)]
        share = tile // cap
        return halo_ref.at[
            index // share, pl.ds(pl.multiple_of((index % share) * cap, cap), cap)
        ]

    def halo_source(index):
        if cap >= tile:
            return out_buf.at[pl.ds(index * (cap // tile), cap // tile)]
        share = tile // cap
        return out_buf.at[
            index // share, pl.ds(pl.multiple_of((index % share) * cap, cap), cap)
        ]

    def halo_copy(peer, mark):
        return remote(
            halo_source(peer),
            halo_place(mark),
            halo_send.at[peer],
            halo_recv.at[mark],
            {"dom": peer},
        )

    def req_copy(peer, mark):
        return remote(myreq, reqs.at[mark], req_send.at[peer], req_recv.at[mark], {"scen": peer})

    def loc_copy(peer, mark):
        return remote(
            stage.at[pl.ds(peer * per, per)],
            local_ref.at[pl.ds(mark * per, per)],
            loc_send.at[peer],
            loc_recv.at[mark],
            {"scen": peer},
        )

    def d1_copy(peer, mark):
        return remote(
            mine, block(gat1, mark, PAD), d1_send.at[peer], d1_recv.at[mark], {"dom": peer}
        )

    doubling = []
    held, mask = [0], n_scen // 2
    while mask:
        doubling.append([(mask, k) for k in held])
        held, mask = held + [k + mask for k in held], mask // 2

    def doubled(ref, send, recv, mask, k):
        part = block(ref, flipped(s, k), ref.shape[0] // n_scen)
        at = (n_scen // (2 * mask) - 1) + held.index(k)
        return remote(part, part, send.at[at], recv.at[at], {"scen": flipped(s, mask)})

    def arriving(ref, send, recv, mask, k):
        part = block(ref, flipped(s, k + mask), ref.shape[0] // n_scen)
        at = (n_scen // (2 * mask) - 1) + held.index(k)
        return remote(part, part, send.at[at], recv.at[at], {"scen": flipped(s, mask)})

    both_weights = ((w1f_ref, w1_send, w1_recv), (w2f_ref, w2_send, w2_recv))
    drivers = ((gat2, d2_send, d2_recv),)

    def start_step(arrays, step):
        for mask, k in doubling[step]:
            for array in arrays:
                doubled(*array, mask, k).start()

    def wait_step(arrays, step):
        for mask, k in doubling[step]:
            for array in arrays:
                arriving(*array, mask, k).wait_recv()

    def sent(arrays):
        for steps in doubling:
            for mask, k in steps:
                for array in arrays:
                    doubled(*array, mask, k).wait_send()

    loads = {}

    def load(name, src, dst):
        loads[name] = pltpu.make_async_copy(src, dst, in_sem.at[len(loads)])
        loads[name].start()

    load("slot", slot_hbm, slot_ref)
    load("w1", w1_hbm, block(w1f_ref, s, w1_hbm.shape[0]))
    load("w2", w2_hbm, block(w2f_ref, s, w2_hbm.shape[0]))
    load("count", count_hbm, count_ref)
    load("rows", rows_hbm, rows_ref)
    load("hot", hot_hbm, hot_ref)
    quarter = tiles // 4
    for i in range(4):
        piece = pl.ds(i * quarter, quarter)
        load(f"emb{i}", emb_hbm.at[piece], emb_ref.at[piece])

    barrier = pltpu.get_barrier_semaphore()
    dom_peers(
        lambda p: pl.semaphore_signal(
            barrier, inc=1, device_id={"dom": p}, device_id_type=MESH
        )
    )
    scen_peers(
        lambda u: pl.semaphore_signal(
            barrier, inc=1, device_id={"scen": u}, device_id_type=MESH
        )
    )

    load("feats", feats_hbm, feats_ref)
    load("fw", fw_hbm, fw_ref)
    load("b1", b1_hbm, b1_ref)
    load("dw", dw_hbm, dw_ref)
    load("adj", adj_hbm, adj_ref)

    square = (LANES, LANES)
    lane = iota_f32(square, 1)
    sub = iota_f32(square, 0)

    padrow[...] = jnp.full(padrow.shape, -1, jnp.int32)
    loads["slot"].wait()
    padrow[0:1, 0:tiles] = slot_ref[...]
    across = jnp.broadcast_to(padrow[0:1, :], square)
    down = across.T
    ilane = lax.broadcasted_iota(jnp.int32, square, 1)
    isub = lax.broadcasted_iota(jnp.int32, square, 0)

    def holder(slots):
        found = jnp.where(slots >= 0, 0, -1)
        for u in range(1, n_scen):
            found = found + jnp.where(slots >= u * tiles, 1, 0)
        return found

    own_a, own_d = holder(across), holder(down)
    same = own_a == own_d
    rank_col = jnp.sum(jnp.where(same & (ilane < isub), 1, 0), axis=1, keepdims=True)
    rank_row = jnp.sum(jnp.where(same & (isub < ilane), 1, 0), axis=0, keepdims=True)
    key_col = jnp.where(isub < tiles, own_d * per + rank_col, -1)
    wanted = jnp.sum(
        jnp.where(key_col == ilane, down - own_d * tiles, 0), axis=0, keepdims=True
    )
    myreq[...] = jnp.broadcast_to(wanted, myreq.shape)
    keys_ref[...] = jnp.broadcast_to(own_a[0:1, :] * per + rank_row, keys_ref.shape)

    pl.semaphore_wait(barrier, n_dom - 1 + n_scen - 1)
    scen_peers(lambda u: req_copy(u, s).start())
    loads["w1"].wait()
    loads["w2"].wait()
    start_step(both_weights, 0)

    for name in ("count", "rows", "hot", "emb0", "emb1", "emb2", "emb3"):
        loads[name].wait()

    def row_of(index, columns):
        block_of = rows_ref[:, columns]
        at = lax.broadcasted_iota(jnp.int32, block_of.shape, 0)
        return jnp.sum(jnp.where(at == index, block_of, 0), axis=0, keepdims=True)

    def halo_group(group):
        first = group * per_group
        columns = []
        for half in range(GROUP // LANES):
            if cap >= LANES:
                parts = cap // LANES
                assert per_group == 1 and parts == GROUP // LANES
                row = row_of(first, slice(half * LANES, (half + 1) * LANES))
                limit = count_ref[first]
                place = lax.broadcasted_iota(jnp.int32, (1, LANES), 1) + half * LANES
                row = jnp.where(place < limit, row, -1)
            else:
                parts = LANES // cap
                row = row_of(group * (GROUP // LANES) + half, slice(0, LANES))
                place = lax.broadcasted_iota(jnp.int32, (1, LANES), 1)
                live = place < 0
                for i in range(parts):
                    limit = count_ref[first + half * parts + i]
                    live = live | ((place >= i * cap) & (place < i * cap + limit) & (place < (i + 1) * cap))
                row = jnp.where(live, row, -1)
            columns.append(spread(row)[1])
        out_buf[pl.ds(group * (GROUP // LANES), GROUP // LANES)] = picked_rows(
            jnp.concatenate(columns, axis=0), emb_ref
        ).reshape(GROUP // LANES, LANES, width)

    def halo_start(group):
        halo_group(group)
        if per_group == 1:
            halo_copy(group, d).start()
            return

        def step(i, carry):
            p = group * per_group + i

            @pl.when(p != d)
            def _():
                halo_copy(p, d).start()

            return carry

        lax.fori_loop(0, per_group, step, 0)

    my_group = d // per_group
    half_way = n_groups // 2
    order = []
    for k in range(half_way - 1, 0, -1):
        far, near = flipped(my_group, k + half_way), flipped(my_group, k)
        order.append(far + (near - far) * (s % 2))
        order.append(near + (far - near) * (s % 2))
    order.append(flipped(my_group, half_way))
    halo_start(order[0])

    scen_peers(lambda u: req_copy(u, u).wait_recv())
    reqs[pl.ds(s, 1)] = myreq[...][None]
    fetch = pltpu.make_async_copy(reqs, reqs_smem, own_sem.at[0])
    fetch.start()
    fetch.wait()

    def stage_for(u):
        for r in range(per):
            slot = reqs_smem[u, 0, s * per + r]
            stage[pl.ds(u * per + r, 1)] = emb_ref[slot][None]

    def serve(u):
        stage_for(u)
        loc_copy(u, s).start()

    scen_peers(serve)
    stage_for(s)
    local_ref[pl.ds(s * per, per)] = stage[pl.ds(s * per, per)]

    halo_start(order[1])

    r_ids, c_ids = spread(hot_ref[...])
    r_own, c_own = whole_part(r_ids, rows), whole_part(c_ids, rows)
    equal = r_ids == c_ids
    new_col = 1.0 - jnp.max(jnp.where(equal & (lane < sub), 1.0, 0.0), axis=1, keepdims=True)
    new_row = 1.0 - jnp.max(jnp.where(equal & (sub < lane), 1.0, 0.0), axis=0, keepdims=True)
    alike = r_own == c_own
    hot_rank_row = jnp.sum(
        jnp.where(alike & (c_ids < r_ids), new_col, 0.0), axis=0, keepdims=True
    )
    hot_rank_col = jnp.sum(
        jnp.where(alike & (r_ids < c_ids), new_row, 0.0), axis=1, keepdims=True
    )
    me = (d * n_scen + s).astype(jnp.float32)
    own_rows = picked_rows(c_ids - me * float(rows), emb_ref)
    chosen = jnp.where(
        (iota_f32((PAD, LANES), 0) == hot_rank_row) & (r_own[0:1, :] == me), new_row, 0.0
    ).astype(jnp.bfloat16)
    mine[...] = jnp.dot(chosen, own_rows, preferred_element_type=jnp.float32).astype(jnp.bfloat16)
    block(gat1, d, PAD)[...] = mine[...]
    dom_peers(lambda p: d1_copy(p, d).start())

    for group in order[2:]:
        halo_start(group)
    if per_group == 1:
        halo_group(my_group)
    else:
        halo_start(my_group)
    own_halo = pltpu.make_async_copy(halo_source(d), halo_place(d), own_sem.at[2])
    own_halo.start()

    wait_step(both_weights, 0)
    start_step(both_weights, 1)

    dom_peers(lambda p: d1_copy(p, p).wait_recv())
    at_row = iota_f32((drv_rows, n_dom * PAD), 0)
    at_dom = whole_part(at_row, hot_cap)
    keep = at_dom * float(PAD) + (at_row - at_dom * float(hot_cap))
    keep = jnp.where(keep == iota_f32(keep.shape, 1), 1.0, 0.0).astype(jnp.bfloat16)
    block(gat2, s, drv_rows)[...] = jnp.dot(
        keep, gat1[...], preferred_element_type=jnp.float32
    ).astype(jnp.bfloat16)
    for step in range(len(doubling)):
        start_step(drivers, step)
        wait_step(drivers, step)
    c_dom = whole_part(c_own, n_scen)
    place = (c_own - c_dom * float(n_scen)) * float(drv_rows) + c_dom * float(hot_cap) + hot_rank_col
    total = jnp.zeros(drv_ref.shape, jnp.float32)
    for at in range(0, n_scen * drv_rows, LANES):
        pick = jnp.where(place == lane + float(at), 1.0, 0.0).astype(jnp.bfloat16)
        total += jnp.dot(pick, gat2[at : at + LANES, :], preferred_element_type=jnp.float32)
    drv_ref[...] = total.astype(jnp.bfloat16)


    for step in range(1, len(doubling)):
        wait_step(both_weights, step)
        if step + 1 < len(doubling):
            start_step(both_weights, step + 1)
    for name in ("feats", "fw", "b1", "dw", "adj"):
        loads[name].wait()
    count = 4 if tiles % 4 == 0 else 1
    part = count * tile

    def own_part(i, carry):
        here = pl.ds(pl.multiple_of(i * part, part), part)
        inner = jnp.dot(
            emb_ref[pl.ds(i * count, count)].reshape(part, width),
            w1f_ref[:width, :],
            preferred_element_type=jnp.float32,
        )
        inner += lax.dot_general(
            feats_ref[:, here],
            fw_ref[...],
            (((0,), (0,)), ((), ())),
            preferred_element_type=jnp.float32,
        )
        inner_ref[here, :] = inner + b1_ref[...]
        return carry

    lax.fori_loop(0, tiles // count, own_part, 0)

    scen_peers(lambda u: loc_copy(u, u).wait())
    to_out = [
        pltpu.make_async_copy(w1f_ref.at[pl.ds(width, width)], w1b_hbm, own_sem.at[3]),
        pltpu.make_async_copy(w2f_ref, w2f_hbm, own_sem.at[4]),
    ]
    for copy in to_out:
        copy.start()
    keys_copy = pltpu.make_async_copy(keys_ref, keys_smem, own_sem.at[1])
    keys_copy.start()
    keys_copy.wait()

    def inner_copy(i):
        here = pl.ds(pl.multiple_of(i * part, part), part)
        return pltpu.make_async_copy(inner_ref.at[here], inner_hbm.at[here], inner_sem.at[i])

    def local_part(i, carry):
        here = pl.ds(pl.multiple_of(i * part, part), part)
        totals = []
        for j in range(count):
            t = i * count + j
            weights = jnp.concatenate([adj_ref[t, 0], dw_ref[t]], axis=1)
            sources = jnp.concatenate([local_ref[keys_smem[0, t]], drv_ref[...]], axis=0)
            total = jnp.dot(weights, sources, preferred_element_type=jnp.float32)
            totals.append(total.astype(jnp.bfloat16))
        inner_ref[here, :] += jnp.dot(
            jnp.concatenate(totals, axis=0),
            w1f_ref[width:, :],
            preferred_element_type=jnp.float32,
        )
        inner_copy(i).start()
        return carry

    lax.fori_loop(0, tiles // count, local_part, 0)

    dom_peers(lambda p: d1_copy(p, p).wait_send())
    scen_peers(lambda u: req_copy(u, u).wait_send())
    sent(both_weights)
    sent(drivers)
    own_halo.wait()
    for copy in to_out:
        copy.wait()

    def finish(i, carry):
        inner_copy(i).wait()
        return carry

    lax.fori_loop(0, tiles // count, finish, 0)
    dom_peers(lambda p: halo_copy(p, p).wait())


def gelu(x):
    size = jnp.abs(x)
    t = 1.0 / (1.0 + (0.3275911 * 0.5**0.5) * size)
    tail = 0.5 * 1.061405429
    for factor in (-1.453152027, 1.421413741, -0.284496736, 0.254829592):
        tail = tail * t + 0.5 * factor
    tail = tail * t * jnp.exp2(x * x * (-0.5 * 1.4426950408889634))
    return jnp.maximum(x, 0.0) - size * tail


def update_kernel(
    slot_ref,
    emb_hbm,
    adj_hbm,
    inner_hbm,
    halo_hbm,
    w1b_hbm,
    w2_hbm,
    b2_ref,
    out_hbm,
    emb_ref,
    adj_ref,
    inner_ref,
    halo_ref,
    w1b_ref,
    w2_ref,
    result_ref,
    part_sem,
    halo_sem,
    weight_sem,
    out_sem,
):
    tiles, tile, _ = adj_ref.shape
    count = 4 if tiles % 4 == 0 else 1
    part = count * tile
    steps = tiles // count

    def started(src, dst, sem):
        copy = pltpu.make_async_copy(src, dst, sem)
        copy.start()
        return copy

    quarter = halo_ref.shape[0] // 4
    ready = []
    for i in range(4):
        here = pl.ds(i * quarter, quarter)
        ready.append(started(halo_hbm.at[here], halo_ref.at[here], halo_sem.at[i]))
    parts = []
    for i in range(steps):
        here = pl.ds(i * part, part)
        some = pl.ds(i * count, count)
        parts.append(
            (
                started(adj_hbm.at[some, 1], adj_ref.at[some], part_sem.at[0, i]),
                started(inner_hbm.at[here], inner_ref.at[here], part_sem.at[1, i]),
                started(emb_hbm.at[here], emb_ref.at[here], part_sem.at[2, i]),
            )
        )
        if i == 0:
            ready.append(started(w1b_hbm, w1b_ref, weight_sem.at[0]))
            ready.append(started(w2_hbm, w2_ref, weight_sem.at[1]))
    for copy in ready:
        copy.wait()
    copies = []
    for i in range(steps):
        for copy in parts[i]:
            copy.wait()
        here = slice(i * part, (i + 1) * part)
        totals = []
        for t in range(i * count, (i + 1) * count):
            total = jnp.dot(adj_ref[t], halo_ref[slot_ref[t]], preferred_element_type=jnp.float32)
            totals.append(total.astype(jnp.bfloat16))
        inner = inner_ref[here, :] + jnp.dot(
            jnp.concatenate(totals, axis=0), w1b_ref[...], preferred_element_type=jnp.float32
        )
        activated = gelu(inner).astype(jnp.bfloat16)
        result = jnp.dot(activated, w2_ref[...], preferred_element_type=jnp.float32)
        own = emb_ref[here, :].astype(jnp.float32) + b2_ref[...]
        result_ref[here, :] = (result + own).astype(jnp.bfloat16)
        copies.append(started(result_ref.at[here], out_hbm.at[here], out_sem.at[i]))
    for copy in copies:
        copy.wait()


def update(halo_slot, embedding, adjacency, inner, halo, w1b, w2, b2):
    rows, width = embedding.shape
    tiles, _, tile, _ = adjacency.shape
    steps = tiles // (4 if tiles % 4 == 0 else 1)
    anywhere = pl.BlockSpec(memory_space=pl.ANY)
    vmem, dma = pltpu.VMEM, pltpu.SemaphoreType.DMA
    return pl.pallas_call(
        update_kernel,
        out_shape=jax.ShapeDtypeStruct((rows, width), jnp.bfloat16),
        in_specs=[pl.BlockSpec(memory_space=pltpu.SMEM)]
        + [anywhere] * 6
        + [pl.BlockSpec(memory_space=pltpu.VMEM)],
        out_specs=anywhere,
        scratch_shapes=[
            vmem(embedding.shape, jnp.bfloat16),
            vmem((tiles, tile, tile), jnp.bfloat16),
            vmem(inner.shape, jnp.float32),
            vmem(halo.shape, jnp.bfloat16),
            vmem(w1b.shape, jnp.bfloat16),
            vmem(w2.shape, jnp.bfloat16),
            vmem((rows, width), jnp.bfloat16),
            dma((3, steps)),
            dma((4,)),
            dma((2,)),
            dma((steps,)),
        ],
        compiler_params=pltpu.CompilerParams(vmem_limit_bytes=60 * 1024 * 1024),
        name="update",
    )(halo_slot, embedding, adjacency, inner, halo, w1b, w2, b2)


def per_device(
    embedding,
    scenario_feats,
    adjacency,
    driver_weight,
    local_slot,
    halo_slot,
    send_rows,
    send_count,
    hot_ids,
    first_weight,
    feature_weight,
    first_bias,
    second_weight,
    second_bias,
):
    n_dom, n_scen = lax.axis_size("dom"), lax.axis_size("scen")
    rows, width = embedding.shape
    tiles, _, tile, _ = adjacency.shape
    slots, cap = send_rows.size, send_rows.shape[1]
    hot = hot_ids.shape[0]
    hot_cap = -(-hot // (n_dom * n_scen))
    assert hot_cap <= PAD and tile == LANES
    if cap < LANES:
        send_rows = send_rows.reshape(-1, LANES)
    bf16, f32, i32 = jnp.bfloat16, jnp.float32, jnp.int32
    vmem, smem, dma = pltpu.VMEM, pltpu.SMEM, pltpu.SemaphoreType.DMA
    anywhere = pl.BlockSpec(memory_space=pl.ANY)
    operands = (
        hot_ids.reshape(1, -1),
        local_slot.reshape(1, -1),
        send_rows,
        send_count,
        embedding.reshape(tiles, tile, width),
        scenario_feats,
        adjacency,
        driver_weight.reshape(tiles, tile, hot),
        first_weight,
        feature_weight,
        first_bias.reshape(1, -1),
        second_weight,
    )
    by_dom = [dma((n_dom,)), dma((n_dom,))]
    by_scen = [dma((n_scen,)), dma((n_scen,))]
    halo, inner, w1b, w2 = pl.pallas_call(
        functools.partial(gather_kernel, n_dom, n_scen, cap, hot_cap),
        out_shape=(
            jax.ShapeDtypeStruct((slots // tile, tile, width), bf16),
            jax.ShapeDtypeStruct((rows, width), f32),
            jax.ShapeDtypeStruct((width, width), bf16),
            jax.ShapeDtypeStruct((width, width), bf16),
        ),
        in_specs=[anywhere] * len(operands),
        out_specs=(anywhere,) * 4,
        scratch_shapes=[
            vmem((1, hot), i32),
            vmem((1, tiles), i32),
            vmem(send_rows.shape, i32),
            smem(send_count.shape, i32),
            vmem((tiles, tile, width), bf16),
            vmem(scenario_feats.shape, bf16),
            vmem(adjacency.shape, bf16),
            vmem((tiles, tile, hot), bf16),
            vmem(feature_weight.shape, bf16),
            vmem((1, width), f32),
            vmem((n_scen * first_weight.shape[0], width), bf16),
            vmem((n_scen * second_weight.shape[0], width), bf16),
            vmem((tiles, tile, width), bf16),
            vmem((hot, width), bf16),
            vmem((8, LANES), i32),
            smem((8, LANES), i32),
            vmem((slots // tile, tile, width), bf16),
            vmem((tiles, tile, width), bf16),
            vmem((8, LANES), i32),
            vmem((n_scen, 8, LANES), i32),
            smem((n_scen, 8, LANES), i32),
            vmem((PAD, width), bf16),
            vmem((n_dom * PAD, width), bf16),
            vmem((n_scen * n_dom * hot_cap, width), bf16),
            vmem((8, LANES), i32),
            vmem((rows, width), f32),
            dma((len(operands) + 3,)),
            *by_dom,
            *by_scen,
            *by_scen,
            *by_dom,
            *by_scen,
            *by_scen,
            *by_scen,
            dma((5,)),
            dma((tiles,)),
        ],
        compiler_params=pltpu.CompilerParams(
            collective_id=0, has_side_effects=True, vmem_limit_bytes=60 * 1024 * 1024
        ),
        name="gather",
    )(*operands)
    return update(
        halo_slot, embedding, adjacency, inner, halo, w1b, w2, second_bias.reshape(1, -1)
    )


def solution(mesh):
    return jax.shard_map(
        per_device,
        mesh=mesh,
        in_specs=(
            P(("dom", "scen"), None),
            P(None, ("dom", "scen")),
            P(("dom", "scen"), None, None, None),
            P(("dom", "scen"), None),
            P(("dom", "scen")),
            P(("dom", "scen")),
            P(("dom", "scen"), None),
            P(("dom", "scen")),
            P(),
            P("scen", None),
            P(),
            P(),
            P("scen", None),
            P(),
        ),
        out_specs=P(("dom", "scen"), None),
        check_vma=False,
    )
```

```python
import functools

import jax
import jax.numpy as jnp
from jax import lax
from jax.experimental import pallas as pl
from jax.experimental.pallas import tpu as pltpu
from jax.sharding import PartitionSpec as P

MESH = pl.DeviceIdType.MESH
LANES = 128
GROUP = 256
PAD = 16


def flipped(index, mask):
    bit = 1
    while bit <= mask:
        if mask & bit:
            index = index + bit * (1 - 2 * ((index // bit) % 2))
        bit *= 2
    return index


def spread(row):
    across = jnp.broadcast_to(row.astype(jnp.float32), (LANES, LANES))
    return across, across.T


def whole_part(values, size):
    return jnp.floor((values + 0.5) * (1.0 / size))


def iota_f32(shape, dim):
    return lax.broadcasted_iota(jnp.int32, shape, dim).astype(jnp.float32)


def picked_rows(column, emb_ref):
    tiles, tile, width = emb_ref.shape
    rows = tiles * tile
    lane = iota_f32(column.shape, 1)
    blocks = [
        jnp.where(column == lane + float(at), 1.0, 0.0).astype(jnp.bfloat16)
        for at in range(0, rows, LANES)
    ]
    return jnp.dot(
        jnp.concatenate(blocks, axis=1),
        emb_ref[...].reshape(rows, width),
        preferred_element_type=jnp.float32,
    ).astype(jnp.bfloat16)


def exchange_kernel(
    n_dom,
    n_scen,
    cap,
    hot_cap,
    ints_ref,
    emb_ref,
    weights_ref,
    halo_ref,
    local_ref,
    drv_ref,
    w1f_ref,
    w2f_ref,
    keys_ref,
    wf_ref,
    out_buf,
    stage,
    myreq,
    reqs,
    reqs_smem,
    mine,
    gat1,
    gat2,
    halo_send,
    halo_recv,
    req_send,
    req_recv,
    loc_send,
    loc_recv,
    d1_send,
    d1_recv,
    d2_send,
    d2_recv,
    wf_send,
    wf_recv,
    own_sem,
):
    d = lax.axis_index("dom")
    s = lax.axis_index("scen")
    tiles, tile, width = emb_ref.shape
    rows = tiles * tile
    per = tiles // n_scen
    per_group = max(1, GROUP // cap)
    n_groups = n_dom // per_group
    drv_rows = n_dom * hot_cap

    def dom_peers(body):
        def step(k, carry):
            body(lax.rem(d + k, n_dom))
            return carry

        lax.fori_loop(1, n_dom, step, 0)

    def scen_peers(body):
        for k in range(n_scen - 1, 0, -1):
            body(flipped(s, k))

    def remote(src, dst, send, recv, where):
        return pltpu.make_async_remote_copy(
            src_ref=src,
            dst_ref=dst,
            send_sem=send,
            recv_sem=recv,
            device_id=where,
            device_id_type=MESH,
        )

    def block(ref, index, size):
        return ref.at[pl.ds(pl.multiple_of(index * size, size), size)]

    def halo_place(index):
        if cap >= tile:
            return halo_ref.at[pl.ds(index * (cap // tile), cap // tile)]
        share = tile // cap
        return halo_ref.at[
            index // share, pl.ds(pl.multiple_of((index % share) * cap, cap), cap)
        ]

    def halo_source(index):
        if cap >= tile:
            return out_buf.at[pl.ds(index * (cap // tile), cap // tile)]
        share = tile // cap
        return out_buf.at[
            index // share, pl.ds(pl.multiple_of((index % share) * cap, cap), cap)
        ]

    def halo_copy(peer, mark):
        return remote(
            halo_source(peer),
            halo_place(mark),
            halo_send.at[peer],
            halo_recv.at[mark],
            {"dom": peer},
        )

    def req_copy(peer, mark):
        return remote(myreq, reqs.at[mark], req_send.at[peer], req_recv.at[mark], {"scen": peer})

    def loc_copy(peer, mark):
        return remote(
            stage.at[pl.ds(peer * per, per)],
            local_ref.at[pl.ds(mark * per, per)],
            loc_send.at[peer],
            loc_recv.at[mark],
            {"scen": peer},
        )

    def d1_copy(peer, mark):
        return remote(
            mine, block(gat1, mark, PAD), d1_send.at[peer], d1_recv.at[mark], {"dom": peer}
        )

    doubling = []
    held, mask = [0], n_scen // 2
    while mask:
        doubling.append([(mask, k) for k in held])
        held, mask = held + [k + mask for k in held], mask // 2

    def doubled(ref, send, recv, mask, k):
        part = block(ref, flipped(s, k), ref.shape[0] // n_scen)
        at = (n_scen // (2 * mask) - 1) + held.index(k)
        return remote(part, part, send.at[at], recv.at[at], {"scen": flipped(s, mask)})

    def arriving(ref, send, recv, mask, k):
        part = block(ref, flipped(s, k + mask), ref.shape[0] // n_scen)
        at = (n_scen // (2 * mask) - 1) + held.index(k)
        return remote(part, part, send.at[at], recv.at[at], {"scen": flipped(s, mask)})

    both_weights = ((wf_ref, wf_send, wf_recv),)
    drivers = ((gat2, d2_send, d2_recv),)

    def start_step(arrays, step):
        for mask, k in doubling[step]:
            for array in arrays:
                doubled(*array, mask, k).start()

    def wait_step(arrays, step):
        for mask, k in doubling[step]:
            for array in arrays:
                arriving(*array, mask, k).wait_recv()

    def sent(arrays):
        for steps in doubling:
            for mask, k in steps:
                for array in arrays:
                    doubled(*array, mask, k).wait_send()

    barrier = pltpu.get_barrier_semaphore()
    dom_peers(
        lambda p: pl.semaphore_signal(
            barrier, inc=1, device_id={"dom": p}, device_id_type=MESH
        )
    )
    scen_peers(
        lambda u: pl.semaphore_signal(
            barrier, inc=1, device_id={"scen": u}, device_id_type=MESH
        )
    )

    square = (LANES, LANES)
    lane = iota_f32(square, 1)
    sub = iota_f32(square, 0)

    n_groups_ints = ints_ref.shape[0] - 1
    across = jnp.broadcast_to(ints_ref[n_groups_ints:, LANES:], square)
    down = across.T
    ilane = lax.broadcasted_iota(jnp.int32, square, 1)
    isub = lax.broadcasted_iota(jnp.int32, square, 0)

    def holder(slots):
        found = jnp.where(slots >= 0, 0, -1)
        for u in range(1, n_scen):
            found = found + jnp.where(slots >= u * tiles, 1, 0)
        return found

    own_a, own_d = holder(across), holder(down)
    same = own_a == own_d
    rank_col = jnp.sum(jnp.where(same & (ilane < isub), 1, 0), axis=1, keepdims=True)
    rank_row = jnp.sum(jnp.where(same & (isub < ilane), 1, 0), axis=0, keepdims=True)
    key_col = jnp.where(isub < tiles, own_d * per + rank_col, -1)
    wanted = jnp.sum(
        jnp.where(key_col == ilane, down - own_d * tiles, 0), axis=0, keepdims=True
    )
    myreq[...] = jnp.broadcast_to(wanted, myreq.shape)
    keys_ref[...] = jnp.broadcast_to(own_a[0:1, :] * per + rank_row, keys_ref.shape)

    pl.semaphore_wait(barrier, n_dom - 1 + n_scen - 1)
    scen_peers(lambda u: req_copy(u, s).start())
    share = weights_ref.shape[0]
    block(wf_ref, s, share)[...] = weights_ref[...]
    start_step(both_weights, 0)

    def row_of(index, columns):
        block_of = ints_ref[:, columns]
        at = lax.broadcasted_iota(jnp.int32, block_of.shape, 0)
        return jnp.sum(jnp.where(at == index, block_of, 0), axis=0, keepdims=True)

    def halo_group(group):
        columns = [
            spread(row_of(group, slice(at, at + LANES)))[1] for at in range(0, GROUP, LANES)
        ]
        out_buf[pl.ds(group * (GROUP // LANES), GROUP // LANES)] = picked_rows(
            jnp.concatenate(columns, axis=0), emb_ref
        ).reshape(GROUP // LANES, LANES, width)

    def halo_start(group):
        halo_group(group)
        if per_group == 1:
            halo_copy(group, d).start()
            return

        def step(i, carry):
            p = group * per_group + i

            @pl.when(p != d)
            def _():
                halo_copy(p, d).start()

            return carry

        lax.fori_loop(0, per_group, step, 0)

    my_group = d // per_group
    half_way = n_groups // 2
    order = []
    for k in range(half_way - 1, 0, -1):
        far, near = flipped(my_group, k + half_way), flipped(my_group, k)
        order.append(far + (near - far) * (s % 2))
        order.append(near + (far - near) * (s % 2))
    order.append(flipped(my_group, half_way))
    halo_start(order[0])

    scen_peers(lambda u: req_copy(u, u).wait_recv())
    reqs[pl.ds(s, 1)] = myreq[...][None]
    fetch = pltpu.make_async_copy(reqs, reqs_smem, own_sem.at[0])
    fetch.start()
    fetch.wait()

    def stage_for(u):
        for r in range(per):
            slot = reqs_smem[u, 0, s * per + r]
            stage[pl.ds(u * per + r, 1)] = emb_ref[slot][None]

    def serve(u):
        stage_for(u)
        loc_copy(u, s).start()

    scen_peers(serve)
    stage_for(s)
    local_ref[pl.ds(s * per, per)] = stage[pl.ds(s * per, per)]

    halo_start(order[1])

    r_ids, c_ids = spread(ints_ref[n_groups_ints:, :LANES])
    r_own, c_own = whole_part(r_ids, rows), whole_part(c_ids, rows)
    equal = r_ids == c_ids
    new_col = 1.0 - jnp.max(jnp.where(equal & (lane < sub), 1.0, 0.0), axis=1, keepdims=True)
    new_row = 1.0 - jnp.max(jnp.where(equal & (sub < lane), 1.0, 0.0), axis=0, keepdims=True)
    alike = r_own == c_own
    hot_rank_row = jnp.sum(
        jnp.where(alike & (c_ids < r_ids), new_col, 0.0), axis=0, keepdims=True
    )
    hot_rank_col = jnp.sum(
        jnp.where(alike & (r_ids < c_ids), new_row, 0.0), axis=1, keepdims=True
    )
    me = (d * n_scen + s).astype(jnp.float32)
    own_rows = picked_rows(c_ids - me * float(rows), emb_ref)
    chosen = jnp.where(
        (iota_f32((PAD, LANES), 0) == hot_rank_row) & (r_own[0:1, :] == me), new_row, 0.0
    ).astype(jnp.bfloat16)
    mine[...] = jnp.dot(chosen, own_rows, preferred_element_type=jnp.float32).astype(jnp.bfloat16)
    block(gat1, d, PAD)[...] = mine[...]
    dom_peers(lambda p: d1_copy(p, d).start())

    for group in order[2:]:
        halo_start(group)
    if per_group == 1:
        halo_group(my_group)
    else:
        halo_start(my_group)
    halo_place(d)[...] = halo_source(d)[...]

    wait_step(both_weights, 0)
    start_step(both_weights, 1)

    dom_peers(lambda p: d1_copy(p, p).wait_recv())
    at_row = iota_f32((drv_rows, n_dom * PAD), 0)
    at_dom = whole_part(at_row, hot_cap)
    keep = at_dom * float(PAD) + (at_row - at_dom * float(hot_cap))
    keep = jnp.where(keep == iota_f32(keep.shape, 1), 1.0, 0.0).astype(jnp.bfloat16)
    block(gat2, s, drv_rows)[...] = jnp.dot(
        keep, gat1[...], preferred_element_type=jnp.float32
    ).astype(jnp.bfloat16)
    for step in range(len(doubling)):
        start_step(drivers, step)
        wait_step(drivers, step)
    c_dom = whole_part(c_own, n_scen)
    place = (c_own - c_dom * float(n_scen)) * float(drv_rows) + c_dom * float(hot_cap) + hot_rank_col
    total = jnp.zeros(drv_ref.shape, jnp.float32)
    for at in range(0, n_scen * drv_rows, LANES):
        pick = jnp.where(place == lane + float(at), 1.0, 0.0).astype(jnp.bfloat16)
        total += jnp.dot(pick, gat2[at : at + LANES, :], preferred_element_type=jnp.float32)
    drv_ref[...] = total.astype(jnp.bfloat16)


    for step in range(1, len(doubling)):
        wait_step(both_weights, step)
        if step + 1 < len(doubling):
            start_step(both_weights, step + 1)
    first = w1f_ref.shape[0] // n_scen
    second = w2f_ref.shape[0] // n_scen
    for u in range(n_scen):
        w1f_ref[u * first : (u + 1) * first, :] = wf_ref[u * share : u * share + first, :]
        w2f_ref[u * second : (u + 1) * second, :] = wf_ref[
            u * share + first : (u + 1) * share, :
        ]

    scen_peers(lambda u: loc_copy(u, u).wait())
    dom_peers(lambda p: d1_copy(p, p).wait_send())
    scen_peers(lambda u: req_copy(u, u).wait_send())
    sent(both_weights)
    sent(drivers)
    dom_peers(lambda p: halo_copy(p, p).wait())


def gelu(x):
    size = jnp.abs(x)
    t = 1.0 / (1.0 + (0.3275911 * 0.5**0.5) * size)
    tail = 0.5 * 1.061405429
    for factor in (-1.453152027, 1.421413741, -0.284496736, 0.254829592):
        tail = tail * t + 0.5 * factor
    tail = tail * t * jnp.exp2(x * x * (-0.5 * 1.4426950408889634))
    return jnp.maximum(x, 0.0) - size * tail


def update_kernel(
    keys_ref,
    slot_ref,
    emb_ref,
    feats_ref,
    adj_ref,
    dw_ref,
    halo_ref,
    local_ref,
    drv_ref,
    w1_ref,
    fw_ref,
    b1_ref,
    w2_ref,
    b2_ref,
    out_hbm,
    result_ref,
    out_sem,
):
    tiles, _, tile, _ = adj_ref.shape
    width = emb_ref.shape[1]
    count = 4 if tiles % 4 == 0 else 1
    part = count * tile
    copies = []
    for i in range(tiles // count):
        here = slice(i * part, (i + 1) * part)
        totals = []
        for t in range(i * count, (i + 1) * count):
            rows = slice(t * tile, (t + 1) * tile)
            weights = jnp.concatenate([adj_ref[t, 0], adj_ref[t, 1]], axis=1)
            sources = jnp.concatenate([local_ref[keys_ref[0, t]], halo_ref[slot_ref[t]]], axis=0)
            total = jnp.dot(weights, sources, preferred_element_type=jnp.float32)
            total += jnp.dot(dw_ref[rows, :], drv_ref[...], preferred_element_type=jnp.float32)
            totals.append(total.astype(jnp.bfloat16))
        own = emb_ref[here, :]
        joined = jnp.concatenate([own, jnp.concatenate(totals, axis=0)], axis=1)
        inner = jnp.dot(joined, w1_ref[...], preferred_element_type=jnp.float32)
        inner += lax.dot_general(
            feats_ref[:, here],
            fw_ref[...],
            (((0,), (0,)), ((), ())),
            preferred_element_type=jnp.float32,
        )
        activated = gelu(inner + b1_ref[...]).astype(jnp.bfloat16)
        result = jnp.dot(activated, w2_ref[...], preferred_element_type=jnp.float32)
        result_ref[here, :] = (result + (own.astype(jnp.float32) + b2_ref[...])).astype(
            jnp.bfloat16
        )
        copies.append(
            pltpu.make_async_copy(result_ref.at[here], out_hbm.at[here], out_sem.at[i])
        )
        copies[-1].start()
    for copy in copies:
        copy.wait()


def update(keys, halo_slot, embedding, *rest):
    rows, width = embedding.shape
    vmem = pl.BlockSpec(memory_space=pltpu.VMEM)
    smem = pl.BlockSpec(memory_space=pltpu.SMEM)
    tiles = halo_slot.shape[0]
    return pl.pallas_call(
        update_kernel,
        out_shape=jax.ShapeDtypeStruct((rows, width), jnp.bfloat16),
        in_specs=[smem, smem, vmem] + [vmem] * len(rest),
        out_specs=pl.BlockSpec(memory_space=pl.ANY),
        scratch_shapes=[
            pltpu.VMEM((rows, width), jnp.bfloat16),
            pltpu.SemaphoreType.DMA((tiles,)),
        ],
        compiler_params=pltpu.CompilerParams(vmem_limit_bytes=20 * 1024 * 1024),
        name="update",
    )(keys, halo_slot, embedding, *rest)


def per_device(
    embedding,
    scenario_feats,
    adjacency,
    driver_weight,
    local_slot,
    halo_slot,
    send_rows,
    send_count,
    hot_ids,
    first_weight,
    feature_weight,
    first_bias,
    second_weight,
    second_bias,
):
    n_dom, n_scen = lax.axis_size("dom"), lax.axis_size("scen")
    rows, width = embedding.shape
    tiles, _, tile, _ = adjacency.shape
    slots, cap = send_rows.size, send_rows.shape[1]
    hot = hot_ids.shape[0]
    hot_cap = -(-hot // (n_dom * n_scen))
    assert hot_cap <= PAD and tile == LANES
    bf16, i32 = jnp.bfloat16, jnp.int32
    vmem, smem, dma = pltpu.VMEM, pltpu.SMEM, pltpu.SemaphoreType.DMA
    live = jnp.arange(cap, dtype=i32)[None, :] < send_count[:, None]
    asked = jnp.concatenate([hot_ids, local_slot, jnp.full((LANES - tiles,), -1, i32)])
    ints = jnp.concatenate(
        [jnp.where(live, send_rows, -1).reshape(-1, GROUP), asked.reshape(1, GROUP)], axis=0
    )
    weights = jnp.concatenate([first_weight, second_weight], axis=0)
    in_vmem = pl.BlockSpec(memory_space=pltpu.VMEM)
    by_dom = [dma((n_dom,)), dma((n_dom,))]
    by_scen = [dma((n_scen,)), dma((n_scen,))]
    halo, local, drivers, w1, w2, keys = pl.pallas_call(
        functools.partial(exchange_kernel, n_dom, n_scen, cap, hot_cap),
        out_shape=(
            jax.ShapeDtypeStruct((slots // tile, tile, width), bf16),
            jax.ShapeDtypeStruct((tiles, tile, width), bf16),
            jax.ShapeDtypeStruct((hot, width), bf16),
            jax.ShapeDtypeStruct((n_scen * first_weight.shape[0], width), bf16),
            jax.ShapeDtypeStruct((n_scen * second_weight.shape[0], width), bf16),
            jax.ShapeDtypeStruct((8, LANES), i32),
        ),
        in_specs=[in_vmem] * 3,
        out_specs=(in_vmem,) * 6,
        scratch_shapes=[
            vmem((n_scen * weights.shape[0], width), bf16),
            vmem((slots // tile, tile, width), bf16),
            vmem((tiles, tile, width), bf16),
            vmem((8, LANES), i32),
            vmem((n_scen, 8, LANES), i32),
            smem((n_scen, 8, LANES), i32),
            vmem((PAD, width), bf16),
            vmem((n_dom * PAD, width), bf16),
            vmem((n_scen * n_dom * hot_cap, width), bf16),
            *by_dom,
            *by_scen,
            *by_scen,
            *by_dom,
            *by_scen,
            *by_scen,
            dma((2,)),
        ],
        compiler_params=pltpu.CompilerParams(
            collective_id=0, has_side_effects=True, vmem_limit_bytes=20 * 1024 * 1024
        ),
        cost_estimate=pl.CostEstimate(
            flops=2 * slots * rows * width, bytes_accessed=64 * rows * width, transcendentals=0
        ),
        name="exchange",
    )(ints, embedding.reshape(tiles, tile, width), weights)
    return update(
        keys,
        halo_slot,
        embedding,
        scenario_feats,
        adjacency,
        driver_weight,
        halo,
        local,
        drivers,
        w1,
        feature_weight,
        first_bias.reshape(1, -1),
        w2,
        second_bias.reshape(1, -1),
    )


def solution(mesh):
    return jax.shard_map(
        per_device,
        mesh=mesh,
        in_specs=(
            P(("dom", "scen"), None),
            P(None, ("dom", "scen")),
            P(("dom", "scen"), None, None, None),
            P(("dom", "scen"), None),
            P(("dom", "scen")),
            P(("dom", "scen")),
            P(("dom", "scen"), None),
            P(("dom", "scen")),
            P(),
            P("scen", None),
            P(),
            P(),
            P("scen", None),
            P(),
        ),
        out_specs=P(("dom", "scen"), None),
        check_vma=False,
    )
```

```python
import functools

import jax
import jax.numpy as jnp
from jax import lax
from jax.experimental import pallas as pl
from jax.experimental.pallas import tpu as pltpu
from jax.sharding import PartitionSpec as P

MESH = pl.DeviceIdType.MESH
LANES = 128
GROUP = 256
PAD = 16


def flipped(index, mask):
    bit = 1
    while bit <= mask:
        if mask & bit:
            index = index + bit * (1 - 2 * ((index // bit) % 2))
        bit *= 2
    return index


def spread(row):
    across = jnp.broadcast_to(row.astype(jnp.float32), (LANES, LANES))
    return across, across.T


def whole_part(values, size):
    return jnp.floor((values + 0.5) * (1.0 / size))


def iota_f32(shape, dim):
    return lax.broadcasted_iota(jnp.int32, shape, dim).astype(jnp.float32)


def picked_rows(column, emb_ref):
    tiles, tile, width = emb_ref.shape
    rows = tiles * tile
    lane = iota_f32(column.shape, 1)
    blocks = [
        jnp.where(column == lane + float(at), 1.0, 0.0).astype(jnp.bfloat16)
        for at in range(0, rows, LANES)
    ]
    return jnp.dot(
        jnp.concatenate(blocks, axis=1),
        emb_ref[...].reshape(rows, width),
        preferred_element_type=jnp.float32,
    ).astype(jnp.bfloat16)


def gather_kernel(
    n_dom,
    n_scen,
    cap,
    hot_cap,
    hot_hbm,
    slot_hbm,
    rows_hbm,
    count_hbm,
    emb_hbm,
    feats_hbm,
    adj_hbm,
    dw_hbm,
    w1_hbm,
    fw_hbm,
    b1_hbm,
    w2_hbm,
    halo_ref,
    inner_hbm,
    w1b_hbm,
    w2f_hbm,
    hot_ref,
    slot_ref,
    rows_ref,
    count_ref,
    emb_ref,
    feats_ref,
    adj_ref,
    dw_ref,
    fw_ref,
    b1_ref,
    w1f_ref,
    w2f_ref,
    local_ref,
    drv_ref,
    keys_ref,
    keys_smem,
    out_buf,
    stage,
    myreq,
    reqs,
    reqs_smem,
    mine,
    gat1,
    gat2,
    padrow,
    inner_ref,
    in_sem,
    halo_send,
    halo_recv,
    req_send,
    req_recv,
    loc_send,
    loc_recv,
    d1_send,
    d1_recv,
    d2_send,
    d2_recv,
    w1_send,
    w1_recv,
    w2_send,
    w2_recv,
    own_sem,
    inner_sem,
):
    d = lax.axis_index("dom")
    s = lax.axis_index("scen")
    tiles, tile, width = emb_ref.shape
    rows = tiles * tile
    per = tiles // n_scen
    per_group = max(1, GROUP // cap)
    n_groups = n_dom // per_group
    drv_rows = n_dom * hot_cap

    def dom_peers(body):
        def step(k, carry):
            body(lax.rem(d + k, n_dom))
            return carry

        lax.fori_loop(1, n_dom, step, 0)

    def scen_peers(body):
        for k in range(n_scen - 1, 0, -1):
            body(flipped(s, k))

    def remote(src, dst, send, recv, where):
        return pltpu.make_async_remote_copy(
            src_ref=src,
            dst_ref=dst,
            send_sem=send,
            recv_sem=recv,
            device_id=where,
            device_id_type=MESH,
        )

    def block(ref, index, size):
        return ref.at[pl.ds(pl.multiple_of(index * size, size), size)]

    def halo_place(index):
        if cap >= tile:
            return halo_ref.at[pl.ds(index * (cap // tile), cap // tile)]
        share = tile // cap
        return halo_ref.at[
            index // share, pl.ds(pl.multiple_of((index % share) * cap, cap), cap)
        ]

    def halo_source(index):
        if cap >= tile:
            return out_buf.at[pl.ds(index * (cap // tile), cap // tile)]
        share = tile // cap
        return out_buf.at[
            index // share, pl.ds(pl.multiple_of((index % share) * cap, cap), cap)
        ]

    def halo_copy(peer, mark):
        return remote(
            halo_source(peer),
            halo_place(mark),
            halo_send.at[peer],
            halo_recv.at[mark],
            {"dom": peer},
        )

    def req_copy(peer, mark):
        return remote(myreq, reqs.at[mark], req_send.at[peer], req_recv.at[mark], {"scen": peer})

    def loc_copy(peer, mark):
        return remote(
            stage.at[pl.ds(peer * per, per)],
            local_ref.at[pl.ds(mark * per, per)],
            loc_send.at[peer],
            loc_recv.at[mark],
            {"scen": peer},
        )

    def d1_copy(peer, mark):
        return remote(
            mine, block(gat1, mark, PAD), d1_send.at[peer], d1_recv.at[mark], {"dom": peer}
        )

    doubling = []
    held, mask = [0], n_scen // 2
    while mask:
        doubling.append([(mask, k) for k in held])
        held, mask = held + [k + mask for k in held], mask // 2

    def doubled(ref, send, recv, mask, k):
        part = block(ref, flipped(s, k), ref.shape[0] // n_scen)
        at = (n_scen // (2 * mask) - 1) + held.index(k)
        return remote(part, part, send.at[at], recv.at[at], {"scen": flipped(s, mask)})

    def arriving(ref, send, recv, mask, k):
        part = block(ref, flipped(s, k + mask), ref.shape[0] // n_scen)
        at = (n_scen // (2 * mask) - 1) + held.index(k)
        return remote(part, part, send.at[at], recv.at[at], {"scen": flipped(s, mask)})

    both_weights = ((w1f_ref, w1_send, w1_recv), (w2f_ref, w2_send, w2_recv))
    drivers = ((gat2, d2_send, d2_recv),)

    def start_step(arrays, step):
        for mask, k in doubling[step]:
            for array in arrays:
                doubled(*array, mask, k).start()

    def wait_step(arrays, step):
        for mask, k in doubling[step]:
            for array in arrays:
                arriving(*array, mask, k).wait_recv()

    def sent(arrays):
        for steps in doubling:
            for mask, k in steps:
                for array in arrays:
                    doubled(*array, mask, k).wait_send()

    loads = {}

    def load(name, src, dst):
        loads[name] = pltpu.make_async_copy(src, dst, in_sem.at[len(loads)])
        loads[name].start()

    load("slot", slot_hbm, slot_ref)
    load("w1", w1_hbm, block(w1f_ref, s, w1_hbm.shape[0]))
    load("w2", w2_hbm, block(w2f_ref, s, w2_hbm.shape[0]))
    load("count", count_hbm, count_ref)
    load("rows", rows_hbm, rows_ref)
    load("hot", hot_hbm, hot_ref)
    quarter = tiles // 4
    for i in range(4):
        piece = pl.ds(i * quarter, quarter)
        load(f"emb{i}", emb_hbm.at[piece], emb_ref.at[piece])

    barrier = pltpu.get_barrier_semaphore()
    dom_peers(
        lambda p: pl.semaphore_signal(
            barrier, inc=1, device_id={"dom": p}, device_id_type=MESH
        )
    )
    scen_peers(
        lambda u: pl.semaphore_signal(
            barrier, inc=1, device_id={"scen": u}, device_id_type=MESH
        )
    )

    load("feats", feats_hbm, feats_ref)
    load("fw", fw_hbm, fw_ref)
    load("b1", b1_hbm, b1_ref)
    load("dw", dw_hbm, dw_ref)
    load("adj", adj_hbm, adj_ref)

    square = (LANES, LANES)
    lane = iota_f32(square, 1)
    sub = iota_f32(square, 0)

    padrow[...] = jnp.full(padrow.shape, -1, jnp.int32)
    loads["slot"].wait()
    padrow[0:1, 0:tiles] = slot_ref[...]
    across = jnp.broadcast_to(padrow[0:1, :], square)
    down = across.T
    ilane = lax.broadcasted_iota(jnp.int32, square, 1)
    isub = lax.broadcasted_iota(jnp.int32, square, 0)

    def holder(slots):
        found = jnp.where(slots >= 0, 0, -1)
        for u in range(1, n_scen):
            found = found + jnp.where(slots >= u * tiles, 1, 0)
        return found

    own_a, own_d = holder(across), holder(down)
    same = own_a == own_d
    rank_col = jnp.sum(jnp.where(same & (ilane < isub), 1, 0), axis=1, keepdims=True)
    rank_row = jnp.sum(jnp.where(same & (isub < ilane), 1, 0), axis=0, keepdims=True)
    key_col = jnp.where(isub < tiles, own_d * per + rank_col, -1)
    wanted = jnp.sum(
        jnp.where(key_col == ilane, down - own_d * tiles, 0), axis=0, keepdims=True
    )
    myreq[...] = jnp.broadcast_to(wanted, myreq.shape)
    keys_ref[...] = jnp.broadcast_to(own_a[0:1, :] * per + rank_row, keys_ref.shape)

    pl.semaphore_wait(barrier, n_dom - 1 + n_scen - 1)
    scen_peers(lambda u: req_copy(u, s).start())
    loads["w1"].wait()
    loads["w2"].wait()
    start_step(both_weights, 0)

    for name in ("count", "rows", "hot", "emb0", "emb1", "emb2", "emb3"):
        loads[name].wait()

    def row_of(index, columns):
        block_of = rows_ref[:, columns]
        at = lax.broadcasted_iota(jnp.int32, block_of.shape, 0)
        return jnp.sum(jnp.where(at == index, block_of, 0), axis=0, keepdims=True)

    def halo_group(group):
        first = group * per_group
        columns = []
        for half in range(GROUP // LANES):
            if cap >= LANES:
                parts = cap // LANES
                assert per_group == 1 and parts == GROUP // LANES
                row = row_of(first, slice(half * LANES, (half + 1) * LANES))
                limit = count_ref[first]
                place = lax.broadcasted_iota(jnp.int32, (1, LANES), 1) + half * LANES
                row = jnp.where(place < limit, row, -1)
            else:
                parts = LANES // cap
                row = row_of(group * (GROUP // LANES) + half, slice(0, LANES))
                place = lax.broadcasted_iota(jnp.int32, (1, LANES), 1)
                live = place < 0
                for i in range(parts):
                    limit = count_ref[first + half * parts + i]
                    live = live | ((place >= i * cap) & (place < i * cap + limit) & (place < (i + 1) * cap))
                row = jnp.where(live, row, -1)
            columns.append(spread(row)[1])
        out_buf[pl.ds(group * (GROUP // LANES), GROUP // LANES)] = picked_rows(
            jnp.concatenate(columns, axis=0), emb_ref
        ).reshape(GROUP // LANES, LANES, width)

    def halo_start(group):
        halo_group(group)
        if per_group == 1:
            halo_copy(group, d).start()
            return

        def step(i, carry):
            p = group * per_group + i

            @pl.when(p != d)
            def _():
                halo_copy(p, d).start()

            return carry

        lax.fori_loop(0, per_group, step, 0)

    my_group = d // per_group
    half_way = n_groups // 2
    order = []
    for k in range(half_way - 1, 0, -1):
        far, near = flipped(my_group, k + half_way), flipped(my_group, k)
        order.append(far + (near - far) * (s % 2))
        order.append(near + (far - near) * (s % 2))
    order.append(flipped(my_group, half_way))
    halo_start(order[0])

    scen_peers(lambda u: req_copy(u, u).wait_recv())
    reqs[pl.ds(s, 1)] = myreq[...][None]
    fetch = pltpu.make_async_copy(reqs, reqs_smem, own_sem.at[0])
    fetch.start()
    fetch.wait()

    def stage_for(u):
        for r in range(per):
            slot = reqs_smem[u, 0, s * per + r]
            stage[pl.ds(u * per + r, 1)] = emb_ref[slot][None]

    def serve(u):
        stage_for(u)
        loc_copy(u, s).start()

    scen_peers(serve)
    stage_for(s)
    local_ref[pl.ds(s * per, per)] = stage[pl.ds(s * per, per)]

    halo_start(order[1])

    r_ids, c_ids = spread(hot_ref[...])
    r_own, c_own = whole_part(r_ids, rows), whole_part(c_ids, rows)
    equal = r_ids == c_ids
    new_col = 1.0 - jnp.max(jnp.where(equal & (lane < sub), 1.0, 0.0), axis=1, keepdims=True)
    new_row = 1.0 - jnp.max(jnp.where(equal & (sub < lane), 1.0, 0.0), axis=0, keepdims=True)
    alike = r_own == c_own
    hot_rank_row = jnp.sum(
        jnp.where(alike & (c_ids < r_ids), new_col, 0.0), axis=0, keepdims=True
    )
    hot_rank_col = jnp.sum(
        jnp.where(alike & (r_ids < c_ids), new_row, 0.0), axis=1, keepdims=True
    )
    me = (d * n_scen + s).astype(jnp.float32)
    own_rows = picked_rows(c_ids - me * float(rows), emb_ref)
    chosen = jnp.where(
        (iota_f32((PAD, LANES), 0) == hot_rank_row) & (r_own[0:1, :] == me), new_row, 0.0
    ).astype(jnp.bfloat16)
    mine[...] = jnp.dot(chosen, own_rows, preferred_element_type=jnp.float32).astype(jnp.bfloat16)
    block(gat1, d, PAD)[...] = mine[...]
    dom_peers(lambda p: d1_copy(p, d).start())

    for group in order[2:]:
        halo_start(group)
    if per_group == 1:
        halo_group(my_group)
    else:
        halo_start(my_group)
    own_halo = pltpu.make_async_copy(halo_source(d), halo_place(d), own_sem.at[2])
    own_halo.start()

    wait_step(both_weights, 0)
    start_step(both_weights, 1)

    dom_peers(lambda p: d1_copy(p, p).wait_recv())
    at_row = iota_f32((drv_rows, n_dom * PAD), 0)
    at_dom = whole_part(at_row, hot_cap)
    keep = at_dom * float(PAD) + (at_row - at_dom * float(hot_cap))
    keep = jnp.where(keep == iota_f32(keep.shape, 1), 1.0, 0.0).astype(jnp.bfloat16)
    block(gat2, s, drv_rows)[...] = jnp.dot(
        keep, gat1[...], preferred_element_type=jnp.float32
    ).astype(jnp.bfloat16)
    for step in range(len(doubling)):
        start_step(drivers, step)
        wait_step(drivers, step)
    c_dom = whole_part(c_own, n_scen)
    place = (c_own - c_dom * float(n_scen)) * float(drv_rows) + c_dom * float(hot_cap) + hot_rank_col
    total = jnp.zeros(drv_ref.shape, jnp.float32)
    for at in range(0, n_scen * drv_rows, LANES):
        pick = jnp.where(place == lane + float(at), 1.0, 0.0).astype(jnp.bfloat16)
        total += jnp.dot(pick, gat2[at : at + LANES, :], preferred_element_type=jnp.float32)
    drv_ref[...] = total.astype(jnp.bfloat16)


    for step in range(1, len(doubling)):
        wait_step(both_weights, step)
        if step + 1 < len(doubling):
            start_step(both_weights, step + 1)
    for name in ("feats", "fw", "b1", "dw", "adj"):
        loads[name].wait()
    count = 4 if tiles % 4 == 0 else 1
    part = count * tile

    def own_part(i, carry):
        here = pl.ds(pl.multiple_of(i * part, part), part)
        inner = jnp.dot(
            emb_ref[pl.ds(i * count, count)].reshape(part, width),
            w1f_ref[:width, :],
            preferred_element_type=jnp.float32,
        )
        inner += lax.dot_general(
            feats_ref[:, here],
            fw_ref[...],
            (((0,), (0,)), ((), ())),
            preferred_element_type=jnp.float32,
        )
        inner_ref[here, :] = inner + b1_ref[...]
        return carry

    lax.fori_loop(0, tiles // count, own_part, 0)

    scen_peers(lambda u: loc_copy(u, u).wait())
    to_out = [
        pltpu.make_async_copy(w1f_ref.at[pl.ds(width, width)], w1b_hbm, own_sem.at[3]),
        pltpu.make_async_copy(w2f_ref, w2f_hbm, own_sem.at[4]),
    ]
    for copy in to_out:
        copy.start()
    keys_copy = pltpu.make_async_copy(keys_ref, keys_smem, own_sem.at[1])
    keys_copy.start()
    keys_copy.wait()

    def inner_copy(i):
        here = pl.ds(pl.multiple_of(i * part, part), part)
        return pltpu.make_async_copy(inner_ref.at[here], inner_hbm.at[here], inner_sem.at[i])

    def local_part(i, carry):
        here = pl.ds(pl.multiple_of(i * part, part), part)
        totals = []
        for j in range(count):
            t = i * count + j
            weights = jnp.concatenate([adj_ref[t, 0], dw_ref[t]], axis=1)
            sources = jnp.concatenate([local_ref[keys_smem[0, t]], drv_ref[...]], axis=0)
            total = jnp.dot(weights, sources, preferred_element_type=jnp.float32)
            totals.append(total.astype(jnp.bfloat16))
        inner_ref[here, :] += jnp.dot(
            jnp.concatenate(totals, axis=0),
            w1f_ref[width:, :],
            preferred_element_type=jnp.float32,
        )
        inner_copy(i).start()
        return carry

    lax.fori_loop(0, tiles // count, local_part, 0)

    dom_peers(lambda p: d1_copy(p, p).wait_send())
    scen_peers(lambda u: req_copy(u, u).wait_send())
    sent(both_weights)
    sent(drivers)
    own_halo.wait()
    for copy in to_out:
        copy.wait()

    def finish(i, carry):
        inner_copy(i).wait()
        return carry

    lax.fori_loop(0, tiles // count, finish, 0)
    dom_peers(lambda p: halo_copy(p, p).wait())


def update_kernel(
    count,
    slot_ref,
    emb_hbm,
    adj_hbm,
    inner_hbm,
    halo_hbm,
    w1b_hbm,
    w2_hbm,
    b2_ref,
    out_ref,
    emb_ref,
    adj_ref,
    inner_ref,
    halo_ref,
    w1b_ref,
    w2_ref,
    part_sem,
    whole_sem,
):
    step = pl.program_id(0)
    part = out_ref.shape[0]
    steps = adj_ref.shape[0] // count

    def part_copies(i):
        here = pl.ds(pl.multiple_of(i * part, part), part)
        some = pl.ds(i * count, count)
        return (
            pltpu.make_async_copy(adj_hbm.at[some, 1], adj_ref.at[some], part_sem.at[0, i]),
            pltpu.make_async_copy(inner_hbm.at[here], inner_ref.at[here], part_sem.at[1, i]),
            pltpu.make_async_copy(emb_hbm.at[here], emb_ref.at[here], part_sem.at[2, i]),
        )

    half = halo_ref.shape[0] // 2
    whole_copies = [
        pltpu.make_async_copy(
            halo_hbm.at[pl.ds(at * half, half)], halo_ref.at[pl.ds(at * half, half)], whole_sem.at[at]
        )
        for at in range(2)
    ]
    whole_copies.append(pltpu.make_async_copy(w1b_hbm, w1b_ref, whole_sem.at[2]))
    whole_copies.append(pltpu.make_async_copy(w2_hbm, w2_ref, whole_sem.at[3]))

    @pl.when(step == 0)
    def _():
        for copy in whole_copies:
            copy.start()
        for i in range(min(2, steps)):
            for copy in part_copies(i):
                copy.start()
        for copy in whole_copies:
            copy.wait()

    @pl.when(step + 2 < steps)
    def _():
        for copy in part_copies(step + 2):
            copy.start()

    for copy in part_copies(step):
        copy.wait()
    here = pl.ds(pl.multiple_of(step * part, part), part)
    totals = []
    for j in range(count):
        t = step * count + j
        total = jnp.dot(adj_ref[t], halo_ref[slot_ref[t]], preferred_element_type=jnp.float32)
        totals.append(total.astype(jnp.bfloat16))
    inner = inner_ref[here, :] + jnp.dot(
        jnp.concatenate(totals, axis=0), w1b_ref[...], preferred_element_type=jnp.float32
    )
    activated = (0.5 * inner * (1.0 + lax.erf(inner * (0.5**0.5)))).astype(jnp.bfloat16)
    result = jnp.dot(activated, w2_ref[...], preferred_element_type=jnp.float32)
    own = emb_ref[here, :].astype(jnp.float32) + b2_ref[...]
    out_ref[...] = (result + own).astype(jnp.bfloat16)


def update(halo_slot, embedding, adjacency, inner, halo, w1b, w2, b2):
    rows, width = embedding.shape
    tiles, _, tile, _ = adjacency.shape
    count = 4 if tiles % 4 == 0 else 1
    steps = tiles // count
    anywhere = pl.BlockSpec(memory_space=pl.ANY)
    vmem, dma = pltpu.VMEM, pltpu.SemaphoreType.DMA
    return pl.pallas_call(
        functools.partial(update_kernel, count),
        grid_spec=pltpu.PrefetchScalarGridSpec(
            num_scalar_prefetch=1,
            grid=(steps,),
            in_specs=[anywhere] * 6 + [pl.BlockSpec(b2.shape, lambda i, *_: (0, 0))],
            out_specs=pl.BlockSpec((count * tile, width), lambda i, *_: (i, 0)),
            scratch_shapes=[
                vmem(embedding.shape, jnp.bfloat16),
                vmem((tiles, tile, tile), jnp.bfloat16),
                vmem(inner.shape, jnp.float32),
                vmem(halo.shape, jnp.bfloat16),
                vmem(w1b.shape, jnp.bfloat16),
                vmem(w2.shape, jnp.bfloat16),
                dma((3, steps)),
                dma((4,)),
            ],
        ),
        out_shape=jax.ShapeDtypeStruct((rows, width), jnp.bfloat16),
        compiler_params=pltpu.CompilerParams(vmem_limit_bytes=60 * 1024 * 1024),
        name="update",
    )(halo_slot, embedding, adjacency, inner, halo, w1b, w2, b2)


def per_device(
    embedding,
    scenario_feats,
    adjacency,
    driver_weight,
    local_slot,
    halo_slot,
    send_rows,
    send_count,
    hot_ids,
    first_weight,
    feature_weight,
    first_bias,
    second_weight,
    second_bias,
):
    n_dom, n_scen = lax.axis_size("dom"), lax.axis_size("scen")
    rows, width = embedding.shape
    tiles, _, tile, _ = adjacency.shape
    slots, cap = send_rows.size, send_rows.shape[1]
    hot = hot_ids.shape[0]
    hot_cap = -(-hot // (n_dom * n_scen))
    assert hot_cap <= PAD and tile == LANES
    if cap < LANES:
        send_rows = send_rows.reshape(-1, LANES)
    bf16, f32, i32 = jnp.bfloat16, jnp.float32, jnp.int32
    vmem, smem, dma = pltpu.VMEM, pltpu.SMEM, pltpu.SemaphoreType.DMA
    anywhere = pl.BlockSpec(memory_space=pl.ANY)
    operands = (
        hot_ids.reshape(1, -1),
        local_slot.reshape(1, -1),
        send_rows,
        send_count,
        embedding.reshape(tiles, tile, width),
        scenario_feats,
        adjacency,
        driver_weight.reshape(tiles, tile, hot),
        first_weight,
        feature_weight,
        first_bias.reshape(1, -1),
        second_weight,
    )
    by_dom = [dma((n_dom,)), dma((n_dom,))]
    by_scen = [dma((n_scen,)), dma((n_scen,))]
    halo, inner, w1b, w2 = pl.pallas_call(
        functools.partial(gather_kernel, n_dom, n_scen, cap, hot_cap),
        out_shape=(
            jax.ShapeDtypeStruct((slots // tile, tile, width), bf16),
            jax.ShapeDtypeStruct((rows, width), f32),
            jax.ShapeDtypeStruct((width, width), bf16),
            jax.ShapeDtypeStruct((width, width), bf16),
        ),
        in_specs=[anywhere] * len(operands),
        out_specs=(anywhere,) * 4,
        scratch_shapes=[
            vmem((1, hot), i32),
            vmem((1, tiles), i32),
            vmem(send_rows.shape, i32),
            smem(send_count.shape, i32),
            vmem((tiles, tile, width), bf16),
            vmem(scenario_feats.shape, bf16),
            vmem(adjacency.shape, bf16),
            vmem((tiles, tile, hot), bf16),
            vmem(feature_weight.shape, bf16),
            vmem((1, width), f32),
            vmem((n_scen * first_weight.shape[0], width), bf16),
            vmem((n_scen * second_weight.shape[0], width), bf16),
            vmem((tiles, tile, width), bf16),
            vmem((hot, width), bf16),
            vmem((8, LANES), i32),
            smem((8, LANES), i32),
            vmem((slots // tile, tile, width), bf16),
            vmem((tiles, tile, width), bf16),
            vmem((8, LANES), i32),
            vmem((n_scen, 8, LANES), i32),
            smem((n_scen, 8, LANES), i32),
            vmem((PAD, width), bf16),
            vmem((n_dom * PAD, width), bf16),
            vmem((n_scen * n_dom * hot_cap, width), bf16),
            vmem((8, LANES), i32),
            vmem((rows, width), f32),
            dma((len(operands) + 3,)),
            *by_dom,
            *by_scen,
            *by_scen,
            *by_dom,
            *by_scen,
            *by_scen,
            *by_scen,
            dma((5,)),
            dma((tiles,)),
        ],
        compiler_params=pltpu.CompilerParams(
            collective_id=0, has_side_effects=True, vmem_limit_bytes=60 * 1024 * 1024
        ),
        name="gather",
    )(*operands)
    return update(
        halo_slot, embedding, adjacency, inner, halo, w1b, w2, second_bias.reshape(1, -1)
    )


def solution(mesh):
    return jax.shard_map(
        per_device,
        mesh=mesh,
        in_specs=(
            P(("dom", "scen"), None),
            P(None, ("dom", "scen")),
            P(("dom", "scen"), None, None, None),
            P(("dom", "scen"), None),
            P(("dom", "scen")),
            P(("dom", "scen")),
            P(("dom", "scen"), None),
            P(("dom", "scen")),
            P(),
            P("scen", None),
            P(),
            P(),
            P("scen", None),
            P(),
        ),
        out_specs=P(("dom", "scen"), None),
        check_vma=False,
    )
```
